512 devices in a mesh: sp: 32 (over z, x_hi), tp: 16 (over x_lo, y, core).
Axes of the slice: x: 4 (x_hi: 2, x_lo: 2; x = x_hi * 2 + x_lo), y: 4, z: 16, core: 2. Of those that a mesh axis runs over, the one named last changes fastest.
Arguments:
- tokens: bfloat16 [2, 128, 32, 3072], P(None, 'sp', None, 'tp'), may hold values from -6 to 6
- qkv_weight: bfloat16 [2, 3072, 3, 2048], P(None, 'sp', None, 'tp'), may hold values from -0.109375 to 0.109375
- out_weight: bfloat16 [2, 2048, 3072], P(None, 'tp', 'sp'), may hold values from -0.125 to 0.125
- norm_gain: float32 [2, 3072], replicated, may hold values from 0.5 to 1.5
- qk_gain: float32 [2, 2, 128], replicated, may hold values from 0.25 to 1.75
- shifts: int32 [2, 2], replicated, may hold values from 0 to 7, as said below
Outputs:
- restored: bfloat16 [2, 128, 32, 3072], P(None, 'sp', None, 'tp')
The draws below stay inside these ranges and needn't reach their ends.
Inputs may be any that keep to these rules, and one draw needn't show every extreme that they name: shifts[1] equals shifts[0] plus 4//2 along rows and 4 along columns, modulo 4 and 8; every column offset is 3 or 7.
All inputs are finite; a program needn't handle non-finite values.
Results may differ from the reference program's by a relative error of at most 0.015.
Values may be sent and summed in bfloat16 or wider, within the bound.
No kernel may reach another device: no remote copies, remote signals or barrier semaphores. Data moves between devices by JAX's collectives and lax.ppermute only.
A program may use at most 64 MiB of HBM per device.

```python
import math
import jax
import jax.numpy as jnp
from jax import lax

D = 3072
HEADS = 16
HDIM = 128
FRAMES = 2
ROWS_DEV = 4
COLS = 32
WH = 4
WW = 8
HEIGHT = 128
N_SP = 32
N_TP = 16


def draw_shifts(key, part):
    key = jax.random.fold_in(key, 11)
    first_key, second_key = jax.random.split(key)
    row_first = jax.random.randint(first_key, (), 0, WH)
    picked = jax.random.randint(second_key, (), 0, 2)
    col_first = WW // 2 - 1 + picked * (WW // 2)
    row_second = (row_first + WH // 2) % WH
    col_second = (col_first + WW // 2) % WW
    first_pair = jnp.stack([row_first, col_first])
    second_pair = jnp.stack([row_second, col_second])
    return jnp.stack([first_pair, second_pair]).astype(jnp.int32)


def steps_of(rng, extent, cuts, least, top_value):
    level, own = 1.0, jax.random.fold_in(rng, 6)
    for axis_at, shards_of in cuts:
        heights = jnp.exp(jax.random.uniform(jax.random.fold_in(own, axis_at), (shards_of,), jnp.float32, least / len(cuts), top_value / len(cuts)))
        level = level * jnp.repeat(heights, extent[axis_at] // shards_of).reshape([-1 if axis == axis_at else 1 for axis in range(len(extent))])
    return level


def normal_values(key, dims, deviation, reach, cuts=(), kind=jnp.bfloat16):
    factor_of = steps_of(key, dims, cuts, -0.22, 0.18) if cuts else 1.0
    entries = jax.random.normal(key, dims, jnp.float32) * deviation * factor_of
    return jnp.minimum(jnp.maximum(entries, -reach), reach).astype(kind)


def setup_inputs(seed: int = 0) -> dict:
    keys = jax.random.split(jax.random.key(seed), 7)
    tokens = normal_values(keys[0], (FRAMES, HEIGHT, COLS, D), 1.0, 6.0, ((1, 32), (3, 16)))
    qkv_weight = normal_values(keys[1], (2, D, 3, HEADS * HDIM), D ** -0.5, 0.109375, ((1, 32), (3, 16)))
    out_weight = normal_values(keys[2], (2, HEADS * HDIM, D), (HEADS * HDIM) ** -0.5, 0.125, ((1, 16), (2, 32)))
    norm_gain = jnp.clip(1.0 + 0.1 * jax.random.normal(keys[3], (2, D), jnp.float32), 0.5, 1.5)
    qk_gain = jnp.clip(1.0 + 0.15 * jax.random.normal(keys[4], (2, 2, HDIM), jnp.float32), 0.25, 1.75)
    shifts = draw_shifts(jax.random.fold_in(keys[6], 71), 0)
    return dict(tokens=tokens, qkv_weight=qkv_weight, out_weight=out_weight, norm_gain=norm_gain, qk_gain=qk_gain, shifts=shifts)


def normalize(inputs, scale_gain):
    mean_square = lax.optimization_barrier(jnp.mean(inputs * inputs, axis=-1, keepdims=True))
    return inputs * lax.rsqrt(mean_square + 1e-06) * scale_gain

def window_mask(first_row, slab_rows, band_rows, slab_cols, frames, total_rows, shift_row, shift_col):
    query_row = first_row + jnp.arange(slab_rows, dtype=jnp.int32)
    key_row = first_row - WH + jnp.arange(band_rows, dtype=jnp.int32)
    column = jnp.arange(slab_cols, dtype=jnp.int32)
    query_win = (query_row + shift_row) // WH
    key_win = (key_row + shift_row) // WH
    column_win = (column + shift_col) // WW
    valid = (key_row >= 0) & (key_row < total_rows)
    same_row = (query_win[:, None] == key_win[None, :]) & valid[None, :]
    same_col = column_win[:, None] == column_win[None, :]
    small = same_row[:, None, :, None] & same_col[None, :, None, :]
    small = small.reshape(slab_rows * slab_cols, band_rows * slab_cols)
    whole = jnp.broadcast_to(small[None, :, None, :], (frames, slab_rows * slab_cols, frames, band_rows * slab_cols))
    return whole.reshape(frames * slab_rows * slab_cols, frames * band_rows * slab_cols).astype(jnp.float32)

def attend_slab(queries, key_rows, value_rows, inside):
    heads = queries.shape[-2]
    head_width = queries.shape[-1]
    flat_queries = queries.reshape(-1, heads, head_width).astype(jnp.float32)
    flat_keys = key_rows.reshape(-1, heads, head_width).astype(jnp.float32)
    flat_values = value_rows.reshape(-1, heads, head_width).astype(jnp.float32)
    scores = jnp.einsum('qhd,khd->hqk', flat_queries, flat_keys) * (1.0 / math.sqrt(head_width))
    weights = jnp.exp(scores) * inside[None]
    normalized = (weights / lax.optimization_barrier(jnp.sum(weights, axis=-1, keepdims=True))).astype(jnp.bfloat16)
    attended = jnp.einsum('hqk,khd->qhd', normalized.astype(jnp.float32), flat_values)
    return attended.astype(jnp.bfloat16).reshape(queries.shape[:3] + (heads * head_width,))

def run_block(current, qkv_block, out_block, gain_block, qk_block, shift_block):
    frames, total_rows, slab_cols, width = current.shape
    current_f = current.astype(jnp.float32)
    normed = normalize(current_f, gain_block).astype(jnp.bfloat16)
    projected = jnp.dot(normed.reshape(-1, width), qkv_block.reshape(width, -1), preferred_element_type=jnp.float32)
    projected = projected.reshape(frames, total_rows, slab_cols, 3, HEADS, HDIM)
    queries = normalize(projected[..., 0, :, :], qk_block[0]).astype(jnp.bfloat16)
    key_rows = normalize(projected[..., 1, :, :], qk_block[1]).astype(jnp.bfloat16)
    value_rows = projected[..., 2, :, :].astype(jnp.bfloat16)
    padding = ((0, 0), (WH, WH), (0, 0), (0, 0), (0, 0))
    key_padded = jnp.pad(key_rows, padding)
    value_padded = jnp.pad(value_rows, padding)
    band_rows = ROWS_DEV + 2 * WH

    def one_slab(slab_index):
        first_row = slab_index * ROWS_DEV
        slab_queries = lax.dynamic_slice_in_dim(queries, first_row, ROWS_DEV, 1)
        slab_keys = lax.dynamic_slice_in_dim(key_padded, first_row, band_rows, 1)
        slab_values = lax.dynamic_slice_in_dim(value_padded, first_row, band_rows, 1)
        inside = window_mask(first_row, ROWS_DEV, band_rows, slab_cols, frames, total_rows, shift_block[0], shift_block[1])
        return attend_slab(slab_queries, slab_keys, slab_values, inside)
    slabs = lax.map(one_slab, jnp.arange(N_SP, dtype=jnp.int32))
    attended = jnp.transpose(slabs, (1, 0, 2, 3, 4)).reshape(-1, HEADS * HDIM)
    group = HEADS * HDIM // N_TP

    def add_group(group_index, running):
        rows_in = lax.dynamic_slice_in_dim(attended, group_index * group, group, 1)
        weight_in = lax.dynamic_slice_in_dim(out_block, group_index * group, group, 0)
        partial_value = jnp.dot(rows_in, weight_in, preferred_element_type=jnp.float32)
        rounded = lax.optimization_barrier(partial_value.astype(jnp.bfloat16))
        return running + rounded.astype(jnp.float32)
    running = lax.fori_loop(0, N_TP, add_group, jnp.zeros((attended.shape[0], width), jnp.float32))
    return (current_f + running.reshape(current.shape)).astype(jnp.bfloat16)

def reference(tokens, qkv_weight, out_weight, norm_gain, qk_gain, shifts):
    current = tokens
    for which_block in range(2):
        current = run_block(current, qkv_weight[which_block], out_weight[which_block], norm_gain[which_block], qk_gain[which_block], shifts[which_block])
    return current
```

```python
import functools
import math

import jax
import jax.numpy as jnp
from jax import lax
from jax.experimental import pallas as pl
from jax.experimental.pallas import tpu as pltpu
from jax.sharding import Mesh, PartitionSpec as P

WH = 4
WW = 8
TP = ("xl", "y", "c")
SP = ("z", "xh")
NT = (((1,), (1,)), ((), ()))
TN = (((0,), (0,)), ((), ()))


def head_attention(projected, row_scale, qk_gain, same_window):
    width = projected.shape[1] // 3

    def normed(part, which):
        rows = projected[:, part * width : (part + 1) * width] * row_scale
        mean_square = jnp.mean(rows * rows, axis=-1, keepdims=True)
        return (rows * lax.rsqrt(mean_square + 1e-06) * qk_gain[which : which + 1, :]).astype(
            jnp.bfloat16
        )

    queries, key_rows = normed(0, 0), normed(1, 1)
    value_rows = (projected[:, 2 * width :] * row_scale).astype(jnp.bfloat16)
    scores = lax.dot_general(queries, key_rows, NT, preferred_element_type=jnp.float32)
    weights = jnp.where(same_window, jnp.exp(scores * (1.0 / math.sqrt(width))), 0.0)
    weights = (weights / jnp.sum(weights, axis=-1, keepdims=True)).astype(jnp.bfloat16)
    return jnp.dot(weights, value_rows, preferred_element_type=jnp.float32).astype(jnp.bfloat16)


def block_kernel(
    slab_rows, half_cols, total_rows, total_cols,
    place, x_ref, w_ref, w2_ref, gain_ref, qk_gain_ref, out_ref, scaled_ref,
):
    width, tokens = x_ref.shape
    step = gain_ref.shape[1]
    gains = gain_ref[...].T
    squares = jnp.zeros((step, tokens), jnp.float32)
    for i in range(width // step):
        rows = x_ref[i * step : (i + 1) * step, :].astype(jnp.float32)
        squares = squares + rows * rows
        scaled_ref[:, i * step : (i + 1) * step] = (rows * gains[:, i : i + 1]).T.astype(
            jnp.bfloat16
        )
    mean_square = jnp.sum(squares, axis=0, keepdims=True) * (1.0 / width)
    row_scale = jnp.broadcast_to(lax.rsqrt(mean_square + 1e-06), (8, tokens)).T[:, 0:1]

    first_row, shift_row, shift_col, first_col = place[0], place[1], place[2], place[3]

    def window(axis):
        token = lax.broadcasted_iota(jnp.int32, (tokens, tokens), axis)
        col = first_col + lax.bitwise_and(token, half_cols - 1)
        row = lax.bitwise_and(
            lax.shift_right_logical(token, half_cols.bit_length() - 1), slab_rows - 1
        )
        row = lax.bitwise_and(first_row + row, total_rows - 1)
        col = jnp.where(col < shift_col, col + total_cols, col)
        row_window = lax.shift_right_logical(row + shift_row, WH.bit_length() - 1)
        return row_window * 16 + lax.shift_right_logical(col, WW.bit_length() - 1)

    same_window = window(0) == window(1)
    heads = []
    for ref in (w_ref, w2_ref):
        head = qk_gain_ref.shape[1]
        projected = jnp.dot(
            scaled_ref[...], ref[:, : 3 * head], preferred_element_type=jnp.float32
        )
        heads.append(head_attention(projected, row_scale, qk_gain_ref[...], same_window))
    chunk = 512
    for i in range(width // chunk):
        rows = slice(i * chunk, (i + 1) * chunk)
        total = jnp.zeros((chunk, tokens), jnp.float32)
        for ref, attended in zip((w_ref, w2_ref), heads):
            total = total + lax.dot_general(
                ref[rows, 3 * head :], attended, NT, preferred_element_type=jnp.float32
            )
        out_ref[rows, :] = total.astype(jnp.bfloat16)


def run_block(dims, place, x_t, w, w2, gain, qk_gain):
    width, tokens = x_t.shape
    vmem = pl.BlockSpec(memory_space=pltpu.VMEM)
    return pl.pallas_call(
        functools.partial(block_kernel, *dims),
        out_shape=jax.ShapeDtypeStruct((width, tokens), jnp.bfloat16),
        in_specs=[pl.BlockSpec(memory_space=pltpu.SMEM)] + [vmem] * 5,
        out_specs=vmem,
        scratch_shapes=[pltpu.VMEM((tokens, width), jnp.bfloat16)],
        compiler_params=pltpu.CompilerParams(vmem_limit_bytes=32 * 1024 * 1024),
        cost_estimate=pl.CostEstimate(
            flops=2 * tokens * width * 2 * w.shape[1],
            bytes_accessed=4 * width * w.shape[1] + 4 * width * tokens,
            transcendentals=2 * tokens * tokens,
        ),
        name="window_block",
    )(place, x_t, w, w2, gain, qk_gain)


def neighbour(x, distance):
    count = lax.axis_size(SP)
    return lax.ppermute(x, SP, [(i, (i - distance) % count) for i in range(count)])


def swap_cores(x):
    return lax.ppermute(x, "c", [(0, 1), (1, 0)])


def on_device(tokens, qkv_weight, out_weight, norm_gain, qk_gain, shifts):
    frames, slab_rows, cols, local = tokens.shape
    count = frames * slab_rows * cols
    half = count // 2
    half_cols = cols // 2
    tp_count = lax.axis_size(TP)
    width = local * tp_count
    head = qk_gain.shape[-1]
    total_rows = slab_rows * lax.axis_size(SP)
    sp_rank = lax.axis_index(SP)
    core = lax.axis_index("c")

    shard = jnp.concatenate(
        [
            part
            for b in range(2)
            for part in (qkv_weight[b].reshape(-1, 3 * head), out_weight[b].T)
        ],
        axis=1,
    )
    pair = lax.all_gather(shard, "xh", axis=0, tiled=True)
    gathered = lax.all_gather(pair, "z", axis=0, tiled=True)
    own = [gathered[:, b * 4 * head : (b + 1) * 4 * head] for b in range(2)]
    other = [swap_cores(w) for w in own]

    offset = [shifts[1, 0] + slab_rows // 2, shifts[1, 0]]
    lane = jnp.arange(count, dtype=jnp.int32)
    nat_f, nat_r, nat_w = lane // (slab_rows * cols), lane // cols % slab_rows, lane % cols
    pos_f = lane // (slab_rows * half_cols) % frames
    pos_r = lane // half_cols % slab_rows
    pos_j = lane // half * half_cols + lane % half_cols

    def pick(rows_f, rows_r, rows_c, f, r, c):
        hit = (rows_f[:, None] == f[None]) & (rows_r[:, None] == r[None])
        return (hit & (rows_c[:, None] == c[None])).astype(jnp.bfloat16)

    def place(b):
        first_row = slab_rows * sp_rank - offset[b] + total_rows
        return jnp.stack(
            [first_row, shifts[b, 0], shifts[b, 1], core * half_cols]
        ).astype(jnp.int32)

    dims = (slab_rows, half_cols, total_rows, cols)

    def block(x_t, b):
        pieces = jnp.stack([x_t[:, :half], x_t[:, half:]])
        pieces = jnp.broadcast_to(pieces[None], (tp_count // 2, 2, local, half))
        pieces = pieces.reshape(tp_count, local, half)
        full = lax.all_to_all(pieces, TP, 0, 0, tiled=True).reshape(width, half)
        partial_value = run_block(
            dims, place(b), full, own[b], other[b],
            norm_gain[b].reshape(-1, 128), qk_gain[b],
        )
        parts = lax.all_to_all(
            partial_value.reshape(tp_count, local, half), TP, 0, 0, tiled=True
        )
        parts = parts.reshape(tp_count // 2, 2, local, half).astype(jnp.float32)
        total = jnp.sum(parts, axis=0)
        total = jnp.concatenate([total[0], total[1]], axis=1)
        return (x_t.astype(jnp.float32) + total).astype(jnp.bfloat16)

    def exact(terms, dims_):
        total = sum(
            lax.dot_general(a, b, dims_, preferred_element_type=jnp.float32) for a, b in terms
        )
        return total.astype(jnp.bfloat16)

    natural = tokens.reshape(count, local)
    before = neighbour(natural, -1)
    last_row = neighbour(tokens[:, -1].reshape(frames * cols, local), -2)
    from_before = slab_rows - offset[0] + pos_r
    pos_w = (pos_j - shifts[0, 1]) % cols
    edge = jnp.arange(frames * cols, dtype=jnp.int32)
    x_t = exact(
        [
            (natural, pick(nat_f, nat_r, nat_w, pos_f, from_before - slab_rows, pos_w)),
            (before, pick(nat_f, nat_r, nat_w, pos_f, from_before, pos_w)),
            (last_row, pick(edge // cols, edge * 0 - 1, edge % cols, pos_f, from_before, pos_w)),
        ],
        TN,
    )
    x_t = block(x_t, 0)

    after = neighbour(x_t, 1)
    old_j = (pos_j - shifts[1, 1] + shifts[0, 1]) % cols
    moved = pos_r + slab_rows // 2
    nn = (((1,), (0,)), ((), ()))
    x_t = exact(
        [
            (x_t, pick(pos_f, pos_r, pos_j, pos_f, moved, old_j)),
            (after, pick(pos_f, pos_r, pos_j, pos_f, moved - slab_rows, old_j)),
        ],
        nn,
    )
    x_t = block(x_t, 1)

    after = neighbour(x_t, 1)
    new_j = (nat_w + shifts[1, 1]) % cols
    moved = nat_r + offset[1]
    result = exact(
        [
            (pick(nat_f, moved, new_j, pos_f, pos_r, pos_j), x_t),
            (pick(nat_f, moved - slab_rows, new_j, pos_f, pos_r, pos_j), after),
        ],
        NT,
    )
    return result.reshape(frames, slab_rows, cols, local)


def solution(mesh):
    shape = mesh.devices.shape
    fine = Mesh(mesh.devices.reshape(shape[0] // 2, 2, 2, shape[1] // 4, 2), SP + TP)
    placed = (
        P(None, SP, None, TP),
        P(None, SP, None, TP),
        P(None, TP, SP),
        P(),
        P(),
        P(),
    )
    return jax.shard_map(
        on_device, mesh=fine, in_specs=placed, out_specs=P(None, SP, None, TP), check_vma=False
    )
```

```python
import functools
import math

import jax
import jax.numpy as jnp
from jax import lax
from jax.experimental import pallas as pl
from jax.experimental.pallas import tpu as pltpu
from jax.sharding import Mesh, PartitionSpec as P

WH = 4
WW = 8
TP = ("xl", "y", "c")
SP = ("z8", "z2", "xh")
NT = (((1,), (1,)), ((), ()))
TN = (((0,), (0,)), ((), ()))


def head_attention(projected, row_scale, qk_gain, same_window):
    width = projected.shape[1] // 3

    def normed(part, which):
        rows = projected[:, part * width : (part + 1) * width] * row_scale
        mean_square = jnp.mean(rows * rows, axis=-1, keepdims=True)
        return (rows * lax.rsqrt(mean_square + 1e-06) * qk_gain[which : which + 1, :]).astype(
            jnp.bfloat16
        )

    queries, key_rows = normed(0, 0), normed(1, 1)
    value_rows = (projected[:, 2 * width :] * row_scale).astype(jnp.bfloat16)
    scores = lax.dot_general(queries, key_rows, NT, preferred_element_type=jnp.float32)
    weights = jnp.where(same_window, jnp.exp(scores * (1.0 / math.sqrt(width))), 0.0)
    weights = (weights / jnp.sum(weights, axis=-1, keepdims=True)).astype(jnp.bfloat16)
    return jnp.dot(weights, value_rows, preferred_element_type=jnp.float32).astype(jnp.bfloat16)


def block_kernel(dims, heads, groups, place, key, x_ref, qk_gain_ref, *refs):
    slab_rows, half_cols, total_rows, total_cols = dims
    weights, (out_ref, x_rows_ref) = refs[: heads * groups], refs[heads * groups :]
    slabs, outer, inner, rows, tokens = x_ref.shape
    head = qk_gain_ref.shape[1]
    part = outer * inner * rows // groups
    per = inner // groups

    def window(first_row, axis):
        token = lax.broadcasted_iota(jnp.int32, (tokens, tokens), axis)
        col = key[2] + lax.bitwise_and(token, half_cols - 1)
        row = lax.bitwise_and(
            lax.shift_right_logical(token, half_cols.bit_length() - 1), slab_rows - 1
        )
        row = lax.bitwise_and(first_row + row, total_rows - 1)
        col = jnp.where(col < key[1], col + total_cols, col)
        row_window = lax.shift_right_logical(row + key[0], WH.bit_length() - 1)
        return row_window * 16 + lax.shift_right_logical(col, WW.bit_length() - 1)

    scales = []
    for slab in range(slabs):
        squares = jnp.zeros((rows, tokens), jnp.float32)
        for g in range(groups):
            for i in range(per):
                for o in range(outer):
                    where = i if per == inner else place[g]
                    block = x_ref[slab, o, where].astype(jnp.float32)
                    squares = squares + block * block
        mean_square = jnp.sum(squares, axis=0, keepdims=True) * (1.0 / (outer * inner * rows))
        scales.append(jnp.broadcast_to(lax.rsqrt(mean_square + 1e-06), (8, tokens)).T[:, 0:1])
    for slab in range(slabs):
        for g in range(groups):
            if per == inner:
                block = x_ref[slab].reshape(part, tokens)
            else:
                block = x_ref[slab, :, place[g]].reshape(part, tokens)
            x_rows_ref[slab * tokens : (slab + 1) * tokens, g * part : (g + 1) * part] = block.T

    attended = []
    for h in range(heads):
        projected = jnp.zeros((slabs * tokens, 3 * head), jnp.float32)
        for g in range(groups):
            projected = projected + jnp.dot(
                x_rows_ref[:, g * part : (g + 1) * part],
                weights[h * groups + g][:, : 3 * head],
                preferred_element_type=jnp.float32,
            )
        rows_of = []
        for slab in range(slabs):
            first_row = key[3 + slab]
            rows_of.append(
                head_attention(
                    projected[slab * tokens : (slab + 1) * tokens],
                    scales[slab],
                    qk_gain_ref[...],
                    window(first_row, 0) == window(first_row, 1),
                )
            )
        attended.append(jnp.concatenate(rows_of, axis=0) if slabs > 1 else rows_of[0])
    chunk = part // 2
    for g in range(groups):
        for piece in range(2):
            total = jnp.zeros((chunk, slabs * tokens), jnp.float32)
            for h in range(heads):
                total = total + lax.dot_general(
                    weights[h * groups + g][piece * chunk : (piece + 1) * chunk, 3 * head :],
                    attended[h],
                    NT,
                    preferred_element_type=jnp.float32,
                )
            total = total.astype(jnp.bfloat16)
            span = outer // 2
            for slab in range(slabs):
                block = total[:, slab * tokens : (slab + 1) * tokens]
                where = slice(piece * span, (piece + 1) * span)
                if per == inner:
                    out_ref[slab, where] = block.reshape(span, inner, rows, tokens)
                else:
                    out_ref[slab, where, place[g]] = block.reshape(span, rows, tokens)


def run_block(dims, place, key, x, qk_gain, weights):
    slabs, outer, inner, rows, tokens = x.shape
    heads, groups = len(weights), len(weights[0])
    flat = [w for of_head in weights for w in of_head]
    features = outer * inner * rows
    vmem = pl.BlockSpec(memory_space=pltpu.VMEM)
    smem = pl.BlockSpec(memory_space=pltpu.SMEM)
    return pl.pallas_call(
        functools.partial(block_kernel, dims, heads, groups),
        out_shape=jax.ShapeDtypeStruct(x.shape, jnp.bfloat16),
        in_specs=[smem, smem] + [vmem] * (2 + len(flat)),
        out_specs=vmem,
        scratch_shapes=[pltpu.VMEM((slabs * tokens, features), jnp.bfloat16)],
        compiler_params=pltpu.CompilerParams(vmem_limit_bytes=32 * 1024 * 1024),
        cost_estimate=pl.CostEstimate(
            flops=2 * slabs * tokens * features * heads * flat[0].shape[1],
            bytes_accessed=2 * sum(w.size for w in flat) + 4 * x.size,
            transcendentals=heads * slabs * tokens * tokens,
        ),
        name="window_block",
    )(place, key, x, qk_gain, *flat)


def neighbour(x, distance):
    count = lax.axis_size(SP)
    return lax.ppermute(x, SP, [(i, (i - distance) % count) for i in range(count)])


def swap_cores(x):
    return lax.ppermute(x, "c", [(0, 1), (1, 0)])


def on_device(tokens, qkv_weight, out_weight, norm_gain, qk_gain, shifts):
    frames, slab_rows, cols, local = tokens.shape
    count = frames * slab_rows * cols
    half = count // 2
    half_cols = cols // 2
    tp_count = lax.axis_size(TP)
    head = qk_gain.shape[-1]
    shard_rows = out_weight.shape[-1]
    z_pairs = lax.axis_size("z8")
    sp_count = lax.axis_size(SP)
    total_rows = slab_rows * sp_count
    sp_rank = lax.axis_index(SP)
    x_hi, z_odd, core = lax.axis_index("xh"), lax.axis_index("z2"), lax.axis_index("c")

    def shard(b):
        gain = lax.dynamic_slice_in_dim(norm_gain[b], sp_rank * shard_rows, shard_rows)
        scaled = qkv_weight[b].reshape(shard_rows, 3 * head).astype(jnp.float32) * gain[:, None]
        return jnp.concatenate([scaled.astype(jnp.bfloat16), out_weight[b].T], axis=1)

    turned = lax.ppermute(
        shard(0), ("xh", "c"), [(xh * 2 + c, c * 2 + xh) for xh in range(2) for c in range(2)]
    )
    mine = shard(1)
    theirs = lax.ppermute(mine, "xh", [(0, 1), (1, 0)])
    pair = jnp.where(
        x_hi == 0,
        jnp.concatenate([mine, theirs], axis=0),
        jnp.concatenate([theirs, mine], axis=0),
    )

    offset = [shifts[1, 0] + slab_rows // 2, shifts[1, 0]]
    lane = jnp.arange(count, dtype=jnp.int32)
    nat_f, nat_r, nat_w = lane // (slab_rows * cols), lane // cols % slab_rows, lane % cols
    pos_f = lane // (slab_rows * half_cols) % frames
    pos_r = lane // half_cols % slab_rows
    pos_j = lane // half * half_cols + lane % half_cols

    def pick(rows_f, rows_r, rows_c, f, r, c):
        hit = (rows_f[:, None] == f[None]) & (rows_r[:, None] == r[None])
        return (hit & (rows_c[:, None] == c[None])).astype(jnp.bfloat16)

    dims = (slab_rows, half_cols, total_rows, cols)

    def key(b, slabs):
        first = [slab_rows * slab - offset[b] + total_rows for slab in slabs]
        return jnp.stack([shifts[b, 0], shifts[b, 1], core * half_cols, *first]).astype(jnp.int32)

    def spread(x_t, copies):
        pieces = jnp.stack([x_t[:, :half], x_t[:, half:]])
        pieces = jnp.broadcast_to(pieces[None], (copies, 2, local, half))
        return pieces.reshape(copies * 2, local, half)

    def add_up(x_t, parts):
        parts = parts.reshape(-1, 2, local, half).astype(jnp.float32)
        total = jnp.sum(parts, axis=0)
        total = jnp.concatenate([total[0], total[1]], axis=1)
        return (x_t.astype(jnp.float32) + total).astype(jnp.bfloat16)

    def exact(terms, dims_):
        total = sum(
            lax.dot_general(a, b, dims_, preferred_element_type=jnp.float32) for a, b in terms
        )
        return total.astype(jnp.bfloat16)

    natural = tokens.reshape(count, local)
    before = neighbour(natural, -1)
    last_row = neighbour(tokens[:, -1].reshape(frames * cols, local), -2)
    from_before = slab_rows - offset[0] + pos_r
    pos_w = (pos_j - shifts[0, 1]) % cols
    edge = jnp.arange(frames * cols, dtype=jnp.int32)
    x_t = exact(
        [
            (natural, pick(nat_f, nat_r, nat_w, pos_f, from_before - slab_rows, pos_w)),
            (before, pick(nat_f, nat_r, nat_w, pos_f, from_before, pos_w)),
            (last_row, pick(edge // cols, edge * 0 - 1, edge % cols, pos_f, from_before, pos_w)),
        ],
        TN,
    )
    pieces = spread(x_t, tp_count)
    pieces, turned, pair = lax.optimization_barrier((pieces, turned, pair))
    full = lax.all_to_all(pieces, ("xh",) + TP, 0, 0, tiled=True)
    gathered = lax.all_gather(pair, ("z8", "z2"), axis=0, tiled=True)
    near = lax.all_gather(turned, "z8", axis=0, tiled=True)
    z_count = 2 * z_pairs
    far = lax.ppermute(
        near,
        ("z8", "z2", "c"),
        [(z * 2 + c, (z + 1 - 2 * c) % z_count * 2 + c) for z in range(z_count) for c in range(2)],
    )
    weights = [near, far, swap_cores(near), swap_cores(far)]
    place = jnp.stack(
        [z_odd * 2 + core, (1 - z_odd) * 2 + core, z_odd * 2 + 1 - core, (1 - z_odd) * 2 + 1 - core]
    ).astype(jnp.int32)
    slab = sp_rank - x_hi
    sums = run_block(
        dims, place, key(0, [slab, slab + 1]),
        full.reshape(2, z_pairs, 4, shard_rows, half), qk_gain[0], [weights],
    )
    parts = lax.all_to_all(
        sums.reshape(2 * tp_count, local, half), ("xh",) + TP, 0, 0, tiled=True
    )
    x_t = add_up(x_t, parts)

    after = neighbour(x_t, 1)
    old_j = (pos_j - shifts[1, 1] + shifts[0, 1]) % cols
    moved = pos_r + slab_rows // 2
    nn = (((1,), (0,)), ((), ()))
    x_t = exact(
        [
            (x_t, pick(pos_f, pos_r, pos_j, pos_f, moved, old_j)),
            (after, pick(pos_f, pos_r, pos_j, pos_f, moved - slab_rows, old_j)),
        ],
        nn,
    )
    full = lax.all_to_all(spread(x_t, tp_count // 2), TP, 0, 0, tiled=True)
    sums = run_block(
        dims, place, key(1, [sp_rank]),
        full.reshape(1, sp_count, 1, shard_rows, half), qk_gain[1],
        [[gathered], [swap_cores(gathered)]],
    )
    parts = lax.all_to_all(sums.reshape(tp_count, local, half), TP, 0, 0, tiled=True)
    x_t = add_up(x_t, parts)

    after = neighbour(x_t, 1)
    new_j = (nat_w + shifts[1, 1]) % cols
    moved = nat_r + offset[1]
    result = exact(
        [
            (pick(nat_f, moved, new_j, pos_f, pos_r, pos_j), x_t),
            (pick(nat_f, moved - slab_rows, new_j, pos_f, pos_r, pos_j), after),
        ],
        NT,
    )
    return result.reshape(frames, slab_rows, cols, local)


def solution(mesh):
    shape = mesh.devices.shape
    fine = Mesh(mesh.devices.reshape(shape[0] // 4, 2, 2, 2, shape[1] // 4, 2), SP + TP)
    placed = (
        P(None, SP, None, TP),
        P(None, SP, None, TP),
        P(None, TP, SP),
        P(),
        P(),
        P(),
    )
    return jax.shard_map(
        on_device, mesh=fine, in_specs=placed, out_specs=P(None, SP, None, TP), check_vma=False
    )
```

```python
import functools
import math

import jax
import jax.numpy as jnp
from jax import lax
from jax.experimental import pallas as pl
from jax.experimental.pallas import tpu as pltpu
from jax.sharding import Mesh, PartitionSpec as P

WH = 4
WW = 8
UNITS = 4
CHUNKS = 4
TP = ("xl", "y", "c")
SP = ("z8", "z2", "xh")
NT = (((1,), (1,)), ((), ()))
TN = (((0,), (0,)), ((), ()))


def head_attention(projected, row_scale, qk_gain, same_window):
    width = projected.shape[1] // 3

    def normed(part, which):
        rows = projected[:, part * width : (part + 1) * width] * row_scale
        mean_square = jnp.mean(rows * rows, axis=-1, keepdims=True)
        return (rows * lax.rsqrt(mean_square + 1e-06) * qk_gain[which : which + 1, :]).astype(
            jnp.bfloat16
        )

    queries, key_rows = normed(0, 0), normed(1, 1)
    value_rows = (projected[:, 2 * width :] * row_scale).astype(jnp.bfloat16)
    scores = lax.dot_general(queries, key_rows, NT, preferred_element_type=jnp.float32)
    weights = jnp.where(same_window, jnp.exp(scores * (1.0 / math.sqrt(width))), 0.0)
    weights = (weights / jnp.sum(weights, axis=-1, keepdims=True)).astype(jnp.bfloat16)
    return jnp.dot(weights, value_rows, preferred_element_type=jnp.float32).astype(jnp.bfloat16)


def block_kernel(spec, weights_are_pairs, shifts, x_ref, qk_gain_ref, *refs):
    copies = []
    if weights_are_pairs:
        source, out_ref, x_rows_ref, held_ref, sems = refs
        weights = [held_ref]
        size = source.shape[0] // CHUNKS
        for h in range(source.shape[1]):
            for n in range(CHUNKS):
                there = slice(n * size, (n + 1) * size)
                copies.append(
                    pltpu.make_async_copy(
                        source.at[there, h], held_ref.at[there, h], sems.at[h * CHUNKS + n]
                    )
                )
                copies[-1].start()
    else:
        weights, (out_ref, x_rows_ref) = refs[:-2], refs[-2:]
    slabs, units, rows, tokens = out_ref.shape
    heads = spec.heads
    windows = spec.windows
    head = qk_gain_ref.shape[1]
    step = UNITS * rows
    part = units // (CHUNKS if weights_are_pairs else len(weights))
    order = spec.order()
    shift_row, shift_col = shifts[spec.block, 0], shifts[spec.block, 1]
    first_rows = spec.first_rows(shifts)
    first_col = lax.axis_index("c") * spec.half_cols

    def weight(h, u, count, columns):
        if weights_are_pairs:
            per = weights[0].shape[2] // rows
            found = weights[0][u // per : (u + count) // per, h, :, columns]
            return found.reshape(count * rows, found.shape[-1])
        g, start = u // part, u % part * rows
        return weights[g][start : start + count * rows, columns]

    def window(first_row, axis):
        token = lax.broadcasted_iota(jnp.int32, (tokens, tokens), axis)
        col = first_col + lax.bitwise_and(token, spec.half_cols - 1)
        row = lax.bitwise_and(
            lax.shift_right_logical(token, spec.half_cols.bit_length() - 1), spec.slab_rows - 1
        )
        row = lax.bitwise_and(first_row + row, spec.total_rows - 1)
        col = jnp.where(col < shift_col, col + spec.total_cols, col)
        row_window = lax.shift_right_logical(row + shift_row, WH.bit_length() - 1)
        return row_window * 16 + lax.shift_right_logical(col, WW.bit_length() - 1)

    scales = []
    for w in range(windows):
        squares = jnp.zeros((rows, tokens), jnp.float32)
        for k in range(units):
            block = x_ref[spec.unit(w, k)].astype(jnp.float32)
            squares = squares + block * block
        mean_square = jnp.sum(squares, axis=0, keepdims=True) * (1.0 / (units * rows))
        scales.append(jnp.broadcast_to(lax.rsqrt(mean_square + 1e-06), (8, tokens)).T[:, 0:1])
        for u in range(0, units, UNITS):
            block = jnp.concatenate(
                [x_ref[spec.unit(w, order[u + k])] for k in range(UNITS)], axis=0
            )
            x_rows_ref[w * tokens : (w + 1) * tokens, u * rows : u * rows + step] = block.T

    attended = []
    for h in range(heads):
        projected = jnp.zeros((windows * tokens, 3 * head), jnp.float32)
        for u in range(0, units, part):
            if copies:
                copies[h * CHUNKS + u // part].wait()
            projected = projected + jnp.dot(
                x_rows_ref[:, u * rows : (u + part) * rows],
                weight(h, u, part, slice(0, 3 * head)),
                preferred_element_type=jnp.float32,
            )
        of_window = []
        for w in range(windows):
            first_row = first_rows[w]
            of_window.append(
                head_attention(
                    projected[w * tokens : (w + 1) * tokens],
                    scales[w],
                    qk_gain_ref[...],
                    window(first_row, 0) == window(first_row, 1),
                )
            )
        if windows > slabs:
            frame = tokens // spec.frames
            of_window = [
                of_window[s + (q % 2)][
                    q // 2 * frame + (1 - q % 2) * frame // 2 :
                    q // 2 * frame + (2 - q % 2) * frame // 2
                ]
                for s in range(slabs)
                for q in range(2 * spec.frames)
            ]
        attended.append(jnp.concatenate(of_window, axis=0))
    for u in range(0, units, UNITS):
        total = jnp.zeros((step, slabs * tokens), jnp.float32)
        for h in range(heads):
            total = total + lax.dot_general(
                weight(h, u, UNITS, slice(3 * head, 4 * head)),
                attended[h],
                NT,
                preferred_element_type=jnp.float32,
            )
        total = total.astype(jnp.bfloat16)
        for slab in range(slabs):
            for k in range(UNITS):
                out_ref[slab, order[u + k]] = total[
                    k * rows : (k + 1) * rows, slab * tokens : (slab + 1) * tokens
                ]


class Spec:
    def __init__(self, frames, slab_rows, cols, total_rows):
        self.frames, self.slab_rows, self.half_cols = frames, slab_rows, cols // 2
        self.total_rows, self.total_cols = total_rows, cols


def row_offset(shifts):
    return jnp.where(shifts[1, 0] > WH // 2, shifts[1, 0] - WH, shifts[1, 0])


class First(Spec):
    block, heads, windows, slabs = 0, 1, 3, 2

    def first_rows(self, shifts):
        z = lax.axis_index("z8") * 2 + lax.axis_index("z2")
        first = 2 * self.slab_rows * z - row_offset(shifts) - self.slab_rows // 2
        return [first + self.total_rows + w * self.slab_rows for w in range(self.windows)]

    def unit(self, w, k):
        owner, odd = k >> 1, k & 1
        if w == 1:
            return odd * 48 + owner * 3 + 2
        return (w // 2) * 48 + owner * 3 + odd

    def order(self):
        odd, core = lax.axis_index("z2"), lax.axis_index("c")
        return [
            (2 * m + z) * 2 + x for x in (core, 1 - core) for z in (odd, 1 - odd) for m in range(8)
        ]


class Second(Spec):
    block, heads, windows, slabs = 1, 2, 1, 1

    def first_rows(self, shifts):
        slab = (lax.axis_index("z8") * 2 + lax.axis_index("z2")) * 2 + lax.axis_index("xh")
        return [self.slab_rows * slab - row_offset(shifts) + self.total_rows]

    def unit(self, w, k):
        return k

    def order(self):
        return list(range(32))


def run_block(spec, shifts, x, qk_gain, weights):
    rows, tokens = x.shape[1:]
    units = sum(w.size for w in weights) // (spec.heads * rows * 4 * qk_gain.shape[1])
    scratch = [pltpu.VMEM((spec.windows * tokens, units * rows), jnp.bfloat16)]
    if len(weights) == 1:
        scratch += [
            pltpu.VMEM(weights[0].shape, jnp.bfloat16),
            pltpu.SemaphoreType.DMA((spec.heads * CHUNKS,)),
        ]
    vmem = pl.BlockSpec(memory_space=pltpu.VMEM)
    smem = pl.BlockSpec(memory_space=pltpu.SMEM)
    return pl.pallas_call(
        functools.partial(block_kernel, spec, len(weights) == 1),
        out_shape=jax.ShapeDtypeStruct((spec.slabs, units, rows, tokens), jnp.bfloat16),
        in_specs=[smem, vmem, vmem]
        + [pl.BlockSpec(memory_space=pl.ANY) if len(weights) == 1 else vmem] * len(weights),
        out_specs=vmem,
        scratch_shapes=scratch,
        compiler_params=pltpu.CompilerParams(vmem_limit_bytes=40 * 1024 * 1024),
        cost_estimate=pl.CostEstimate(
            flops=2 * spec.windows * tokens * sum(w.size for w in weights),
            bytes_accessed=2 * sum(w.size for w in weights) + 4 * x.size,
            transcendentals=spec.heads * spec.windows * tokens * tokens,
        ),
        name="window_block",
    )(shifts, x, qk_gain, *weights)


def arrange_kernel(dims, copies, shifts, before_ref, own_ref, after_ref, pieces_ref, x_ref):
    frames, slab_rows, cols = dims
    count, local = own_ref.shape
    half, half_cols = count // 2, cols // 2
    x_hi = lax.axis_index("xh")
    tokens = jnp.concatenate([before_ref[...], own_ref[...], after_ref[...]], axis=0).T
    lane = lax.broadcasted_iota(jnp.int32, (1, count), 1)
    f = lax.bitwise_and(lax.div(lane, slab_rows * half_cols), frames - 1)
    r = lax.bitwise_and(lax.div(lane, half_cols), slab_rows - 1)
    j = lax.div(lane, half) * half_cols + lax.bitwise_and(lane, half_cols - 1)
    w = lax.bitwise_and(j - shifts[0, 1] + cols, cols - 1)

    def rows_from(start):
        row = start - row_offset(shifts) + r
        slab = lax.div(row, slab_rows)
        source = slab * count + f * (slab_rows * cols) + (row - slab * slab_rows) * cols + w
        hit = lax.broadcasted_iota(jnp.int32, (3 * count, count), 0) == source
        chosen = jnp.where(hit, 1.0, 0.0).astype(jnp.bfloat16)
        return jnp.dot(tokens, chosen, preferred_element_type=jnp.float32).astype(jnp.bfloat16)

    outer = rows_from(slab_rows // 2 + slab_rows * x_hi)
    middle = rows_from(slab_rows + slab_rows // 2 - slab_rows * x_hi)
    middle = jnp.where(x_hi == 0, middle[: local // 2], middle[local // 2 :])
    x_ref[...] = rows_from(slab_rows)
    for c in range(2):
        for i in range(copies):
            pieces_ref[2 * i + c, :local] = outer[:, c * half : (c + 1) * half]
            pieces_ref[2 * i + c, local:] = middle[:, c * half : (c + 1) * half]


def arrange(dims, copies, shifts, before, own, after):
    count, local = own.shape
    vmem = pl.BlockSpec(memory_space=pltpu.VMEM)
    return pl.pallas_call(
        functools.partial(arrange_kernel, dims, copies),
        out_shape=(
            jax.ShapeDtypeStruct((2 * copies, local + local // 2, count // 2), jnp.bfloat16),
            jax.ShapeDtypeStruct((local, count), jnp.bfloat16),
        ),
        in_specs=[pl.BlockSpec(memory_space=pltpu.SMEM)] + [vmem] * 3,
        out_specs=(vmem, vmem),
        compiler_params=pltpu.CompilerParams(vmem_limit_bytes=32 * 1024 * 1024),
        cost_estimate=pl.CostEstimate(
            flops=2 * local * 9 * count * count,
            bytes_accessed=2 * (copies + 4) * count * local,
            transcendentals=0,
        ),
        name="arrange_tokens",
    )(shifts, before, own, after)


def neighbour(x, distance):
    count = lax.axis_size(SP)
    return lax.ppermute(x, SP, [(i, (i - distance) % count) for i in range(count)])


def swap_cores(x):
    return lax.ppermute(x, "c", [(0, 1), (1, 0)])


def on_device(tokens, qkv_weight, out_weight, norm_gain, qk_gain, shifts):
    frames, slab_rows, cols, local = tokens.shape
    count = frames * slab_rows * cols
    half = count // 2
    half_cols = cols // 2
    tp_count = lax.axis_size(TP)
    head = qk_gain.shape[-1]
    shard_rows = out_weight.shape[-1]
    sp_count = lax.axis_size(SP)
    total_rows = slab_rows * sp_count
    sp_rank = lax.axis_index(SP)
    x_hi = lax.axis_index("xh")

    def shard(b):
        gain = lax.dynamic_slice_in_dim(norm_gain[b], sp_rank * shard_rows, shard_rows)
        scaled = qkv_weight[b].reshape(shard_rows, 3 * head).astype(jnp.float32) * gain[:, None]
        return jnp.concatenate([scaled.astype(jnp.bfloat16), out_weight[b].T], axis=1)

    turned = lax.ppermute(
        shard(0), ("xh", "c"), [(xh * 2 + c, c * 2 + xh) for xh in range(2) for c in range(2)]
    )
    mine = shard(1)
    theirs = lax.ppermute(mine, "xh", [(0, 1), (1, 0)])
    natural = tokens.reshape(count, local)
    slabs = [neighbour(natural, -1), natural, neighbour(natural, 1)]

    offset = row_offset(shifts)
    lane = jnp.arange(count, dtype=jnp.int32)
    nat_f, nat_r, nat_w = lane // (slab_rows * cols), lane // cols % slab_rows, lane % cols
    pos_f = lane // (slab_rows * half_cols) % frames
    pos_r = lane // half_cols % slab_rows
    pos_j = lane // half * half_cols + lane % half_cols

    def pick(rows_f, rows_r, rows_c, f, r, c):
        hit = (rows_f[:, None] == f[None]) & (rows_r[:, None] == r[None])
        return (hit & (rows_c[:, None] == c[None])).astype(jnp.bfloat16)

    def exact(terms, dims_):
        total = sum(
            lax.dot_general(a, b, dims_, preferred_element_type=jnp.float32) for a, b in terms
        )
        return total.astype(jnp.bfloat16)

    def spread(halves, copies):
        pieces = jnp.broadcast_to(jnp.stack(halves)[None], (copies, 2) + halves[0].shape)
        return pieces.reshape((copies * 2,) + halves[0].shape)

    def add_up(x_t, parts):
        parts = parts.reshape(-1, 2, local, half).astype(jnp.float32)
        total = jnp.sum(parts, axis=0)
        total = jnp.concatenate([total[0], total[1]], axis=1)
        return (x_t.astype(jnp.float32) + total).astype(jnp.bfloat16)

    pieces, x_t = arrange((frames, slab_rows, cols), tp_count, shifts, *slabs)
    pieces, turned = lax.optimization_barrier((pieces, turned))
    full = lax.all_to_all(pieces, ("xh",) + TP, 0, 0, tiled=True)
    near0 = lax.all_gather(turned, "z8", axis=0, tiled=True)
    near0, theirs, full = lax.optimization_barrier((near0, theirs, full))
    pair1 = jnp.where(
        x_hi == 0,
        jnp.concatenate([mine, theirs], axis=0),
        jnp.concatenate([theirs, mine], axis=0),
    )
    gathered1 = lax.all_gather(pair1, ("z8", "z2", "c"), axis=0, tiled=False)
    z_count = sp_count // 2
    far0 = lax.ppermute(
        near0,
        ("z8", "z2", "c"),
        [(z * 2 + c, (z + 1 - 2 * c) % z_count * 2 + c) for z in range(z_count) for c in range(2)],
    )
    sums = run_block(
        First(frames, slab_rows, cols, total_rows), shifts,
        full.reshape(-1, shard_rows, half), qk_gain[0],
        [near0, far0, swap_cores(near0), swap_cores(far0)],
    )
    parts = lax.all_to_all(
        sums.reshape(2 * tp_count, local, half), ("xh",) + TP, 0, 0, tiled=True
    )
    x_t = add_up(x_t, parts)

    old_j = (pos_j - shifts[1, 1] + shifts[0, 1]) % cols
    x_t = exact(
        [(x_t, pick(pos_f, pos_r, pos_j, pos_f, pos_r, old_j))], (((1,), (0,)), ((), ()))
    )
    full = lax.all_to_all(
        spread([x_t[:, :half], x_t[:, half:]], tp_count // 2), TP, 0, 0, tiled=True
    )
    sums = run_block(
        Second(frames, slab_rows, cols, total_rows), shifts,
        full.reshape(-1, shard_rows, half), qk_gain[1],
        [gathered1.reshape(z_count, 2, 2 * shard_rows, 4 * head)],
    )
    parts = lax.all_to_all(sums.reshape(tp_count, local, half), TP, 0, 0, tiled=True)
    x_t = add_up(x_t, parts)

    new_j = (nat_w + shifts[1, 1]) % cols
    moved = nat_r + offset
    result = exact(
        [
            (pick(nat_f, moved - slab_rows * s, new_j, pos_f, pos_r, pos_j), slab)
            for s, slab in ((0, x_t), (1, neighbour(x_t, 1)), (-1, neighbour(x_t, -1)))
        ],
        NT,
    )
    return result.reshape(frames, slab_rows, cols, local)


def solution(mesh):
    shape = mesh.devices.shape
    fine = Mesh(mesh.devices.reshape(shape[0] // 4, 2, 2, 2, shape[1] // 4, 2), SP + TP)
    placed = (
        P(None, SP, None, TP),
        P(None, SP, None, TP),
        P(None, TP, SP),
        P(),
        P(),
        P(),
    )
    return jax.shard_map(
        on_device, mesh=fine, in_specs=placed, out_specs=P(None, SP, None, TP), check_vma=False
    )
```

```python
import functools
import math

import jax
import jax.numpy as jnp
from jax import lax
from jax.experimental import pallas as pl
from jax.experimental.pallas import tpu as pltpu
from jax.sharding import Mesh, PartitionSpec as P

WH = 4
WW = 8
UNITS = 4
CHUNKS = 8
TP = ("xl", "y", "c")
SP = ("z8", "z2", "xh")
NT = (((1,), (1,)), ((), ()))
TN = (((0,), (0,)), ((), ()))


def head_attention(projected, row_scale, qk_gain, same_window):
    width = projected.shape[1] // 3

    def normed(part, which):
        rows = projected[:, part * width : (part + 1) * width] * row_scale
        mean_square = jnp.mean(rows * rows, axis=-1, keepdims=True)
        return (rows * lax.rsqrt(mean_square + 1e-06) * qk_gain[which : which + 1, :]).astype(
            jnp.bfloat16
        )

    queries, key_rows = normed(0, 0), normed(1, 1)
    value_rows = (projected[:, 2 * width :] * row_scale).astype(jnp.bfloat16)
    scores = lax.dot_general(queries, key_rows, NT, preferred_element_type=jnp.float32)
    weights = jnp.where(same_window, jnp.exp(scores * (1.0 / math.sqrt(width))), 0.0)
    weights = (weights / jnp.sum(weights, axis=-1, keepdims=True)).astype(jnp.bfloat16)
    return jnp.dot(weights, value_rows, preferred_element_type=jnp.float32).astype(jnp.bfloat16)


def block_kernel(spec, weights_are_pairs, shifts, x_ref, qk_gain_ref, *refs):
    copies = []
    if weights_are_pairs:
        source, out_ref, x_rows_ref, held_ref, sems = refs
        weights = [held_ref]
        size = source.shape[0] // CHUNKS
        for n in range(CHUNKS):
            there = slice(n * size, (n + 1) * size)
            copies.append(
                pltpu.make_async_copy(source.at[there], held_ref.at[there], sems.at[n])
            )
            copies[-1].start()
    else:
        weights, (out_ref, x_rows_ref) = refs[:-2], refs[-2:]
    slabs, units, rows, tokens = out_ref.shape
    heads = spec.heads
    windows = spec.windows
    head = qk_gain_ref.shape[1]
    step = UNITS * rows
    part = units // (CHUNKS if weights_are_pairs else len(weights))
    order = spec.order()
    shift_row, shift_col = shifts[spec.block, 0], shifts[spec.block, 1]
    first_rows = spec.first_rows(shifts)
    first_col = lax.axis_index("c") * spec.half_cols

    def weight(h, u, count, columns):
        if weights_are_pairs:
            per = weights[0].shape[2] // rows
            found = weights[0][u // per : (u + count) // per, h, :, columns]
            return found.reshape(count * rows, found.shape[-1])
        g, start = u // part, u % part * rows
        return weights[g][start : start + count * rows, columns]

    def window(first_row, axis):
        token = lax.broadcasted_iota(jnp.int32, (tokens, tokens), axis)
        col = first_col + lax.bitwise_and(token, spec.half_cols - 1)
        row = lax.bitwise_and(
            lax.shift_right_logical(token, spec.half_cols.bit_length() - 1), spec.slab_rows - 1
        )
        row = lax.bitwise_and(first_row + row, spec.total_rows - 1)
        col = jnp.where(col < shift_col, col + spec.total_cols, col)
        row_window = lax.shift_right_logical(row + shift_row, WH.bit_length() - 1)
        return row_window * 16 + lax.shift_right_logical(col, WW.bit_length() - 1)

    scales = []
    for w in range(windows):
        squares = jnp.zeros((rows, tokens), jnp.float32)
        for k in range(units):
            block = x_ref[spec.unit(w, k)].astype(jnp.float32)
            squares = squares + block * block
        mean_square = jnp.sum(squares, axis=0, keepdims=True) * (1.0 / (units * rows))
        scales.append(jnp.broadcast_to(lax.rsqrt(mean_square + 1e-06), (8, tokens)).T[:, 0:1])
        for u in range(0, units, UNITS):
            block = jnp.concatenate(
                [x_ref[spec.unit(w, order[u + k])] for k in range(UNITS)], axis=0
            )
            x_rows_ref[w * tokens : (w + 1) * tokens, u * rows : u * rows + step] = block.T

    projected = [jnp.zeros((windows * tokens, 3 * head), jnp.float32)] * heads
    for u in range(0, units, part):
        if copies:
            copies[u // part].wait()
        for h in range(heads):
            projected[h] = projected[h] + jnp.dot(
                x_rows_ref[:, u * rows : (u + part) * rows],
                weight(h, u, part, slice(0, 3 * head)),
                preferred_element_type=jnp.float32,
            )
    attended = []
    for h in range(heads):
        of_window = []
        for w in range(windows):
            first_row = first_rows[w]
            of_window.append(
                head_attention(
                    projected[h][w * tokens : (w + 1) * tokens],
                    scales[w],
                    qk_gain_ref[...],
                    window(first_row, 0) == window(first_row, 1),
                )
            )
        if windows > slabs:
            frame = tokens // spec.frames
            of_window = [
                of_window[s + (q % 2)][
                    q // 2 * frame + (1 - q % 2) * frame // 2 :
                    q // 2 * frame + (2 - q % 2) * frame // 2
                ]
                for s in range(slabs)
                for q in range(2 * spec.frames)
            ]
        attended.append(jnp.concatenate(of_window, axis=0))
    for u in range(0, units, UNITS):
        total = jnp.zeros((step, slabs * tokens), jnp.float32)
        for h in range(heads):
            total = total + lax.dot_general(
                weight(h, u, UNITS, slice(3 * head, 4 * head)),
                attended[h],
                NT,
                preferred_element_type=jnp.float32,
            )
        total = total.astype(jnp.bfloat16)
        for slab in range(slabs):
            for k in range(UNITS):
                out_ref[slab, order[u + k]] = total[
                    k * rows : (k + 1) * rows, slab * tokens : (slab + 1) * tokens
                ]


class Spec:
    def __init__(self, frames, slab_rows, cols, total_rows):
        self.frames, self.slab_rows, self.half_cols = frames, slab_rows, cols // 2
        self.total_rows, self.total_cols = total_rows, cols


def row_offset(shifts):
    return jnp.where(shifts[1, 0] > WH // 2, shifts[1, 0] - WH, shifts[1, 0])


class First(Spec):
    block, heads, windows, slabs = 0, 1, 3, 2

    def first_rows(self, shifts):
        z = lax.axis_index("z8") * 2 + lax.axis_index("z2")
        first = 2 * self.slab_rows * z - row_offset(shifts) - self.slab_rows // 2
        return [first + self.total_rows + w * self.slab_rows for w in range(self.windows)]

    def unit(self, w, k):
        owner, odd = k >> 1, k & 1
        if w == 1:
            return odd * 48 + owner * 3 + 2
        return (w // 2) * 48 + owner * 3 + odd

    def order(self):
        odd, core = lax.axis_index("z2"), lax.axis_index("c")
        return [
            (2 * m + z) * 2 + x for x in (core, 1 - core) for z in (odd, 1 - odd) for m in range(8)
        ]


class Second(Spec):
    block, heads, windows, slabs = 1, 2, 1, 1

    def first_rows(self, shifts):
        slab = (lax.axis_index("z8") * 2 + lax.axis_index("z2")) * 2 + lax.axis_index("xh")
        return [self.slab_rows * slab - row_offset(shifts) + self.total_rows]

    def unit(self, w, k):
        return k

    def order(self):
        return list(range(32))


def run_block(spec, shifts, x, qk_gain, weights):
    rows, tokens = x.shape[1:]
    units = sum(w.size for w in weights) // (spec.heads * rows * 4 * qk_gain.shape[1])
    scratch = [pltpu.VMEM((spec.windows * tokens, units * rows), jnp.bfloat16)]
    if len(weights) == 1:
        scratch += [
            pltpu.VMEM(weights[0].shape, jnp.bfloat16),
            pltpu.SemaphoreType.DMA((CHUNKS,)),
        ]
    vmem = pl.BlockSpec(memory_space=pltpu.VMEM)
    smem = pl.BlockSpec(memory_space=pltpu.SMEM)
    return pl.pallas_call(
        functools.partial(block_kernel, spec, len(weights) == 1),
        out_shape=jax.ShapeDtypeStruct((spec.slabs, units, rows, tokens), jnp.bfloat16),
        in_specs=[smem, vmem, vmem]
        + [pl.BlockSpec(memory_space=pl.ANY) if len(weights) == 1 else vmem] * len(weights),
        out_specs=vmem,
        scratch_shapes=scratch,
        compiler_params=pltpu.CompilerParams(
            vmem_limit_bytes=(58 if len(weights) == 1 else 40) * 1024 * 1024
        ),
        cost_estimate=pl.CostEstimate(
            flops=2 * spec.windows * tokens * sum(w.size for w in weights),
            bytes_accessed=2 * sum(w.size for w in weights) + 4 * x.size,
            transcendentals=spec.heads * spec.windows * tokens * tokens,
        ),
        name="window_block",
    )(shifts, x, qk_gain, *weights)


def arrange_kernel(dims, copies, shifts, before_ref, own_ref, after_ref, pieces_ref, x_ref):
    frames, slab_rows, cols = dims
    count, local = own_ref.shape
    half, half_cols = count // 2, cols // 2
    x_hi = lax.axis_index("xh")
    tokens = jnp.concatenate([before_ref[...], own_ref[...], after_ref[...]], axis=0).T
    lane = lax.broadcasted_iota(jnp.int32, (1, count), 1)
    f = lax.bitwise_and(lax.div(lane, slab_rows * half_cols), frames - 1)
    r = lax.bitwise_and(lax.div(lane, half_cols), slab_rows - 1)
    j = lax.div(lane, half) * half_cols + lax.bitwise_and(lane, half_cols - 1)
    w = lax.bitwise_and(j - shifts[0, 1] + cols, cols - 1)

    def rows_from(start):
        row = start - row_offset(shifts) + r
        slab = lax.div(row, slab_rows)
        source = slab * count + f * (slab_rows * cols) + (row - slab * slab_rows) * cols + w
        hit = lax.broadcasted_iota(jnp.int32, (3 * count, count), 0) == source
        chosen = jnp.where(hit, 1.0, 0.0).astype(jnp.bfloat16)
        return jnp.dot(tokens, chosen, preferred_element_type=jnp.float32).astype(jnp.bfloat16)

    outer = rows_from(slab_rows // 2 + slab_rows * x_hi)
    middle = rows_from(slab_rows + slab_rows // 2 - slab_rows * x_hi)
    middle = jnp.where(x_hi == 0, middle[: local // 2], middle[local // 2 :])
    x_ref[...] = rows_from(slab_rows)
    for c in range(2):
        for i in range(copies):
            pieces_ref[2 * i + c, :local] = outer[:, c * half : (c + 1) * half]
            pieces_ref[2 * i + c, local:] = middle[:, c * half : (c + 1) * half]


def arrange(dims, copies, shifts, before, own, after):
    count, local = own.shape
    vmem = pl.BlockSpec(memory_space=pltpu.VMEM)
    return pl.pallas_call(
        functools.partial(arrange_kernel, dims, copies),
        out_shape=(
            jax.ShapeDtypeStruct((2 * copies, local + local // 2, count // 2), jnp.bfloat16),
            jax.ShapeDtypeStruct((local, count), jnp.bfloat16),
        ),
        in_specs=[pl.BlockSpec(memory_space=pltpu.SMEM)] + [vmem] * 3,
        out_specs=(vmem, vmem),
        compiler_params=pltpu.CompilerParams(vmem_limit_bytes=32 * 1024 * 1024),
        cost_estimate=pl.CostEstimate(
            flops=2 * local * 9 * count * count,
            bytes_accessed=2 * (copies + 4) * count * local,
            transcendentals=0,
        ),
        name="arrange_tokens",
    )(shifts, before, own, after)


def neighbour(x, distance):
    count = lax.axis_size(SP)
    return lax.ppermute(x, SP, [(i, (i - distance) % count) for i in range(count)])


def swap_cores(x):
    return lax.ppermute(x, "c", [(0, 1), (1, 0)])


def on_device(tokens, qkv_weight, out_weight, norm_gain, qk_gain, shifts):
    frames, slab_rows, cols, local = tokens.shape
    count = frames * slab_rows * cols
    half = count // 2
    half_cols = cols // 2
    tp_count = lax.axis_size(TP)
    head = qk_gain.shape[-1]
    shard_rows = out_weight.shape[-1]
    sp_count = lax.axis_size(SP)
    total_rows = slab_rows * sp_count
    sp_rank = lax.axis_index(SP)
    x_hi = lax.axis_index("xh")

    def shard(b):
        gain = lax.dynamic_slice_in_dim(norm_gain[b], sp_rank * shard_rows, shard_rows)
        scaled = qkv_weight[b].reshape(shard_rows, 3 * head).astype(jnp.float32) * gain[:, None]
        return jnp.concatenate([scaled.astype(jnp.bfloat16), out_weight[b].T], axis=1)

    turned = lax.ppermute(
        shard(0), ("xh", "c"), [(xh * 2 + c, c * 2 + xh) for xh in range(2) for c in range(2)]
    )
    mine = shard(1)
    theirs = lax.ppermute(mine, "xh", [(0, 1), (1, 0)])
    natural = tokens.reshape(count, local)
    slabs = [neighbour(natural, -1), natural, neighbour(natural, 1)]

    offset = row_offset(shifts)
    lane = jnp.arange(count, dtype=jnp.int32)
    nat_f, nat_r, nat_w = lane // (slab_rows * cols), lane // cols % slab_rows, lane % cols
    pos_f = lane // (slab_rows * half_cols) % frames
    pos_r = lane // half_cols % slab_rows
    pos_j = lane // half * half_cols + lane % half_cols

    def pick(rows_f, rows_r, rows_c, f, r, c):
        hit = (rows_f[:, None] == f[None]) & (rows_r[:, None] == r[None])
        return (hit & (rows_c[:, None] == c[None])).astype(jnp.bfloat16)

    def exact(terms, dims_):
        total = sum(
            lax.dot_general(a, b, dims_, preferred_element_type=jnp.float32) for a, b in terms
        )
        return total.astype(jnp.bfloat16)

    def spread(halves, copies):
        pieces = jnp.broadcast_to(jnp.stack(halves)[None], (copies, 2) + halves[0].shape)
        return pieces.reshape((copies * 2,) + halves[0].shape)

    def add_up(x_t, parts):
        parts = parts.reshape(-1, 2, local, half).astype(jnp.float32)
        total = jnp.sum(parts, axis=0)
        total = jnp.concatenate([total[0], total[1]], axis=1)
        return (x_t.astype(jnp.float32) + total).astype(jnp.bfloat16)

    pieces, x_t = arrange((frames, slab_rows, cols), tp_count, shifts, *slabs)
    pieces, turned = lax.optimization_barrier((pieces, turned))
    full = lax.all_to_all(pieces, ("xh",) + TP, 0, 0, tiled=True)
    near0 = lax.all_gather(turned, "z8", axis=0, tiled=True)
    near0, theirs, full = lax.optimization_barrier((near0, theirs, full))
    pair1 = jnp.where(
        x_hi == 0,
        jnp.concatenate([mine, theirs], axis=0),
        jnp.concatenate([theirs, mine], axis=0),
    )
    gathered1 = lax.all_gather(pair1, ("z8", "z2", "c"), axis=0, tiled=False)
    z_count = sp_count // 2
    far0 = lax.ppermute(
        near0,
        ("z8", "z2", "c"),
        [(z * 2 + c, (z + 1 - 2 * c) % z_count * 2 + c) for z in range(z_count) for c in range(2)],
    )
    sums = run_block(
        First(frames, slab_rows, cols, total_rows), shifts,
        full.reshape(-1, shard_rows, half), qk_gain[0],
        [near0, far0, swap_cores(near0), swap_cores(far0)],
    )
    parts = lax.all_to_all(
        sums.reshape(2 * tp_count, local, half), ("xh",) + TP, 0, 0, tiled=True
    )
    x_t = add_up(x_t, parts)

    old_j = (pos_j - shifts[1, 1] + shifts[0, 1]) % cols
    x_t = exact(
        [(x_t, pick(pos_f, pos_r, pos_j, pos_f, pos_r, old_j))], (((1,), (0,)), ((), ()))
    )
    full = lax.all_to_all(
        spread([x_t[:, :half], x_t[:, half:]], tp_count // 2), TP, 0, 0, tiled=True
    )
    sums = run_block(
        Second(frames, slab_rows, cols, total_rows), shifts,
        full.reshape(-1, shard_rows, half), qk_gain[1],
        [gathered1.reshape(z_count, 2, 2 * shard_rows, 4 * head)],
    )
    parts = lax.all_to_all(sums.reshape(tp_count, local, half), TP, 0, 0, tiled=True)
    x_t = add_up(x_t, parts)

    new_j = (nat_w + shifts[1, 1]) % cols
    moved = nat_r + offset
    result = exact(
        [
            (pick(nat_f, moved - slab_rows * s, new_j, pos_f, pos_r, pos_j), slab)
            for s, slab in ((0, x_t), (1, neighbour(x_t, 1)), (-1, neighbour(x_t, -1)))
        ],
        NT,
    )
    return result.reshape(frames, slab_rows, cols, local)


def solution(mesh):
    shape = mesh.devices.shape
    fine = Mesh(mesh.devices.reshape(shape[0] // 4, 2, 2, 2, shape[1] // 4, 2), SP + TP)
    placed = (
        P(None, SP, None, TP),
        P(None, SP, None, TP),
        P(None, TP, SP),
        P(),
        P(),
        P(),
    )
    return jax.shard_map(
        on_device, mesh=fine, in_specs=placed, out_specs=P(None, SP, None, TP), check_vma=False
    )
```

```python
import functools
import math

import jax
import jax.numpy as jnp
from jax import lax
from jax.experimental import pallas as pl
from jax.experimental.pallas import tpu as pltpu
from jax.sharding import Mesh, PartitionSpec as P

WH = 4
WW = 8
UNITS = 4
CHUNKS = 4
TP = ("xl", "y", "c")
SP = ("z8", "z2", "xh")
NT = (((1,), (1,)), ((), ()))
TN = (((0,), (0,)), ((), ()))


def head_attention(projected, row_scale, qk_gain, same_window):
    width = projected.shape[1] // 3

    def normed(part, which):
        rows = projected[:, part * width : (part + 1) * width] * row_scale
        mean_square = jnp.mean(rows * rows, axis=-1, keepdims=True)
        return (rows * lax.rsqrt(mean_square + 1e-06) * qk_gain[which : which + 1, :]).astype(
            jnp.bfloat16
        )

    queries, key_rows = normed(0, 0), normed(1, 1)
    value_rows = (projected[:, 2 * width :] * row_scale).astype(jnp.bfloat16)
    scores = lax.dot_general(queries, key_rows, NT, preferred_element_type=jnp.float32)
    weights = jnp.where(same_window, jnp.exp(scores * (1.0 / math.sqrt(width))), 0.0)
    weights = (weights / jnp.sum(weights, axis=-1, keepdims=True)).astype(jnp.bfloat16)
    return jnp.dot(weights, value_rows, preferred_element_type=jnp.float32).astype(jnp.bfloat16)


def block_kernel(spec, weights_are_pairs, shifts, x_ref, qk_gain_ref, *refs):
    copies = []
    if weights_are_pairs:
        source, out_hbm, x_rows_ref, held_ref, x_held, out_ref, sems = refs
        weights = [held_ref]
        fetch = pltpu.make_async_copy(x_ref, x_held, sems.at[CHUNKS])
        fetch.start()
        x_ref = x_held
        size = source.shape[0] // CHUNKS
        for n in range(CHUNKS):
            there = slice(n * size, (n + 1) * size)
            copies.append(
                pltpu.make_async_copy(source.at[there], held_ref.at[there], sems.at[n])
            )
            copies[-1].start()
    else:
        weights, (out_ref, x_rows_ref) = refs[:-2], refs[-2:]
    slabs, units, rows, tokens = out_ref.shape
    heads = spec.heads
    windows = spec.windows
    head = qk_gain_ref.shape[1]
    step = UNITS * rows
    part = units // (CHUNKS if weights_are_pairs else len(weights))
    order = spec.order()
    shift_row, shift_col = shifts[spec.block, 0], shifts[spec.block, 1]
    first_rows = spec.first_rows(shifts)
    first_col = lax.axis_index("c") * spec.half_cols

    def weight(h, u, count, columns):
        if weights_are_pairs:
            per = weights[0].shape[2] // rows
            found = weights[0][u // per : (u + count) // per, h, :, columns]
            return found.reshape(count * rows, found.shape[-1])
        g, start = u // part, u % part * rows
        return weights[g][start : start + count * rows, columns]

    def window(first_row, axis):
        token = lax.broadcasted_iota(jnp.int32, (tokens, tokens), axis)
        col = first_col + lax.bitwise_and(token, spec.half_cols - 1)
        row = lax.bitwise_and(
            lax.shift_right_logical(token, spec.half_cols.bit_length() - 1), spec.slab_rows - 1
        )
        row = lax.bitwise_and(first_row + row, spec.total_rows - 1)
        col = jnp.where(col < shift_col, col + spec.total_cols, col)
        row_window = lax.shift_right_logical(row + shift_row, WH.bit_length() - 1)
        return row_window * 16 + lax.shift_right_logical(col, WW.bit_length() - 1)

    if copies:
        fetch.wait()
    sent = []
    scales = []
    for w in range(windows):
        squares = jnp.zeros((rows, tokens), jnp.float32)
        for k in range(units):
            block = x_ref[spec.unit(w, k)].astype(jnp.float32)
            squares = squares + block * block
        mean_square = jnp.sum(squares, axis=0, keepdims=True) * (1.0 / (units * rows))
        scales.append(jnp.broadcast_to(lax.rsqrt(mean_square + 1e-06), (8, tokens)).T[:, 0:1])
        for u in range(0, units, UNITS):
            block = jnp.concatenate(
                [x_ref[spec.unit(w, order[u + k])] for k in range(UNITS)], axis=0
            )
            x_rows_ref[w * tokens : (w + 1) * tokens, u * rows : u * rows + step] = block.T

    projected = [jnp.zeros((windows * tokens, 3 * head), jnp.float32)] * heads
    for u in range(0, units, part):
        if copies:
            copies[u // part].wait()
        for h in range(heads):
            projected[h] = projected[h] + jnp.dot(
                x_rows_ref[:, u * rows : (u + part) * rows],
                weight(h, u, part, slice(0, 3 * head)),
                preferred_element_type=jnp.float32,
            )
    attended = []
    for h in range(heads):
        of_window = []
        for w in range(windows):
            first_row = first_rows[w]
            of_window.append(
                head_attention(
                    projected[h][w * tokens : (w + 1) * tokens],
                    scales[w],
                    qk_gain_ref[...],
                    window(first_row, 0) == window(first_row, 1),
                )
            )
        if windows > slabs:
            frame = tokens // spec.frames
            of_window = [
                of_window[s + (q % 2)][
                    q // 2 * frame + (1 - q % 2) * frame // 2 :
                    q // 2 * frame + (2 - q % 2) * frame // 2
                ]
                for s in range(slabs)
                for q in range(2 * spec.frames)
            ]
        attended.append(jnp.concatenate(of_window, axis=0))
    for u in range(0, units, UNITS):
        total = jnp.zeros((step, slabs * tokens), jnp.float32)
        for h in range(heads):
            total = total + lax.dot_general(
                weight(h, u, UNITS, slice(3 * head, 4 * head)),
                attended[h],
                NT,
                preferred_element_type=jnp.float32,
            )
        total = total.astype(jnp.bfloat16)
        for slab in range(slabs):
            for k in range(UNITS):
                out_ref[slab, order[u + k]] = total[
                    k * rows : (k + 1) * rows, slab * tokens : (slab + 1) * tokens
                ]
        if copies:
            made = (slice(0, slabs), slice(u, u + UNITS))
            sent.append(
                pltpu.make_async_copy(
                    out_ref.at[made], out_hbm.at[made], sems.at[CHUNKS + 1 + u // UNITS]
                )
            )
            sent[-1].start()
    for copy in sent:
        copy.wait()


class Spec:
    def __init__(self, frames, slab_rows, cols, total_rows):
        self.frames, self.slab_rows, self.half_cols = frames, slab_rows, cols // 2
        self.total_rows, self.total_cols = total_rows, cols


def row_offset(shifts):
    return jnp.where(shifts[1, 0] > WH // 2, shifts[1, 0] - WH, shifts[1, 0])


class First(Spec):
    block, heads, windows, slabs = 0, 1, 3, 2

    def first_rows(self, shifts):
        z = lax.axis_index("z8") * 2 + lax.axis_index("z2")
        first = 2 * self.slab_rows * z - row_offset(shifts) - self.slab_rows // 2
        return [first + self.total_rows + w * self.slab_rows for w in range(self.windows)]

    def unit(self, w, k):
        owner, odd = k >> 1, k & 1
        if w == 1:
            return odd * 48 + owner * 3 + 2
        return (w // 2) * 48 + owner * 3 + odd

    def order(self):
        odd, core = lax.axis_index("z2"), lax.axis_index("c")
        return [
            (2 * m + z) * 2 + x for x in (core, 1 - core) for z in (odd, 1 - odd) for m in range(8)
        ]


class Second(Spec):
    block, heads, windows, slabs = 1, 2, 1, 1

    def first_rows(self, shifts):
        slab = (lax.axis_index("z8") * 2 + lax.axis_index("z2")) * 2 + lax.axis_index("xh")
        return [self.slab_rows * slab - row_offset(shifts) + self.total_rows]

    def unit(self, w, k):
        return k

    def order(self):
        return list(range(32))


def run_block(spec, shifts, x, qk_gain, weights):
    rows, tokens = x.shape[1:]
    units = sum(w.size for w in weights) // (spec.heads * rows * 4 * qk_gain.shape[1])
    scratch = [pltpu.VMEM((spec.windows * tokens, units * rows), jnp.bfloat16)]
    if len(weights) == 1:
        scratch += [
            pltpu.VMEM(weights[0].shape, jnp.bfloat16),
            pltpu.VMEM(x.shape, jnp.bfloat16),
            pltpu.VMEM((spec.slabs, units, rows, tokens), jnp.bfloat16),
            pltpu.SemaphoreType.DMA((CHUNKS + 1 + units // UNITS,)),
        ]
    vmem = pl.BlockSpec(memory_space=pltpu.VMEM)
    smem = pl.BlockSpec(memory_space=pltpu.SMEM)
    place = pl.BlockSpec(memory_space=pl.ANY) if len(weights) == 1 else vmem
    return pl.pallas_call(
        functools.partial(block_kernel, spec, len(weights) == 1),
        out_shape=jax.ShapeDtypeStruct((spec.slabs, units, rows, tokens), jnp.bfloat16),
        in_specs=[smem, place, vmem] + [place] * len(weights),
        out_specs=place,
        scratch_shapes=scratch,
        compiler_params=pltpu.CompilerParams(
            vmem_limit_bytes=(58 if len(weights) == 1 else 40) * 1024 * 1024
        ),
        cost_estimate=pl.CostEstimate(
            flops=2 * spec.windows * tokens * sum(w.size for w in weights),
            bytes_accessed=2 * sum(w.size for w in weights) + 4 * x.size,
            transcendentals=spec.heads * spec.windows * tokens * tokens,
        ),
        name="window_block",
    )(shifts, x, qk_gain, *weights)


def arrange_kernel(dims, copies, shifts, before_ref, own_ref, after_ref, pieces_ref, x_ref):
    frames, slab_rows, cols = dims
    count, local = own_ref.shape
    half, half_cols = count // 2, cols // 2
    x_hi = lax.axis_index("xh")
    tokens = jnp.concatenate([before_ref[...], own_ref[...], after_ref[...]], axis=0).T
    lane = lax.broadcasted_iota(jnp.int32, (1, count), 1)
    f = lax.bitwise_and(lax.div(lane, slab_rows * half_cols), frames - 1)
    r = lax.bitwise_and(lax.div(lane, half_cols), slab_rows - 1)
    j = lax.div(lane, half) * half_cols + lax.bitwise_and(lane, half_cols - 1)
    w = lax.bitwise_and(j - shifts[0, 1] + cols, cols - 1)

    def rows_from(start):
        row = start - row_offset(shifts) + r
        slab = lax.div(row, slab_rows)
        source = slab * count + f * (slab_rows * cols) + (row - slab * slab_rows) * cols + w
        hit = lax.broadcasted_iota(jnp.int32, (3 * count, count), 0) == source
        chosen = jnp.where(hit, 1.0, 0.0).astype(jnp.bfloat16)
        return jnp.dot(tokens, chosen, preferred_element_type=jnp.float32).astype(jnp.bfloat16)

    outer = rows_from(slab_rows // 2 + slab_rows * x_hi)
    middle = rows_from(slab_rows + slab_rows // 2 - slab_rows * x_hi)
    middle = jnp.where(x_hi == 0, middle[: local // 2], middle[local // 2 :])
    x_ref[...] = rows_from(slab_rows)
    for c in range(2):
        for i in range(copies):
            pieces_ref[2 * i + c, :local] = outer[:, c * half : (c + 1) * half]
            pieces_ref[2 * i + c, local:] = middle[:, c * half : (c + 1) * half]


def arrange(dims, copies, shifts, before, own, after):
    count, local = own.shape
    vmem = pl.BlockSpec(memory_space=pltpu.VMEM)
    return pl.pallas_call(
        functools.partial(arrange_kernel, dims, copies),
        out_shape=(
            jax.ShapeDtypeStruct((2 * copies, local + local // 2, count // 2), jnp.bfloat16),
            jax.ShapeDtypeStruct((local, count), jnp.bfloat16),
        ),
        in_specs=[pl.BlockSpec(memory_space=pltpu.SMEM)] + [vmem] * 3,
        out_specs=(vmem, vmem),
        compiler_params=pltpu.CompilerParams(vmem_limit_bytes=32 * 1024 * 1024),
        cost_estimate=pl.CostEstimate(
            flops=2 * local * 9 * count * count,
            bytes_accessed=2 * (copies + 4) * count * local,
            transcendentals=0,
        ),
        name="arrange_tokens",
    )(shifts, before, own, after)


def neighbour(x, distance):
    count = lax.axis_size(SP)
    return lax.ppermute(x, SP, [(i, (i - distance) % count) for i in range(count)])


def swap_cores(x):
    return lax.ppermute(x, "c", [(0, 1), (1, 0)])


def on_device(tokens, qkv_weight, out_weight, norm_gain, qk_gain, shifts):
    frames, slab_rows, cols, local = tokens.shape
    count = frames * slab_rows * cols
    half = count // 2
    half_cols = cols // 2
    tp_count = lax.axis_size(TP)
    head = qk_gain.shape[-1]
    shard_rows = out_weight.shape[-1]
    sp_count = lax.axis_size(SP)
    total_rows = slab_rows * sp_count
    sp_rank = lax.axis_index(SP)
    x_hi = lax.axis_index("xh")

    def shard(b):
        gain = lax.dynamic_slice_in_dim(norm_gain[b], sp_rank * shard_rows, shard_rows)
        scaled = qkv_weight[b].reshape(shard_rows, 3 * head).astype(jnp.float32) * gain[:, None]
        return jnp.concatenate([scaled.astype(jnp.bfloat16), out_weight[b].T], axis=1)

    turned = lax.ppermute(
        shard(0), ("xh", "c"), [(xh * 2 + c, c * 2 + xh) for xh in range(2) for c in range(2)]
    )
    mine = shard(1)
    theirs = lax.ppermute(mine, "xh", [(0, 1), (1, 0)])
    natural = tokens.reshape(count, local)
    slabs = [neighbour(natural, -1), natural, neighbour(natural, 1)]

    offset = row_offset(shifts)
    lane = jnp.arange(count, dtype=jnp.int32)
    nat_f, nat_r, nat_w = lane // (slab_rows * cols), lane // cols % slab_rows, lane % cols
    pos_f = lane // (slab_rows * half_cols) % frames
    pos_r = lane // half_cols % slab_rows
    pos_j = lane // half * half_cols + lane % half_cols

    def pick(rows_f, rows_r, rows_c, f, r, c):
        hit = (rows_f[:, None] == f[None]) & (rows_r[:, None] == r[None])
        return (hit & (rows_c[:, None] == c[None])).astype(jnp.bfloat16)

    def exact(terms, dims_):
        total = sum(
            lax.dot_general(a, b, dims_, preferred_element_type=jnp.float32) for a, b in terms
        )
        return total.astype(jnp.bfloat16)

    def spread(halves, copies):
        pieces = jnp.broadcast_to(jnp.stack(halves)[None], (copies, 2) + halves[0].shape)
        return pieces.reshape((copies * 2,) + halves[0].shape)

    def add_up(x_t, parts):
        parts = parts.reshape(-1, 2, local, half).astype(jnp.float32)
        total = jnp.sum(parts, axis=0)
        total = jnp.concatenate([total[0], total[1]], axis=1)
        return (x_t.astype(jnp.float32) + total).astype(jnp.bfloat16)

    pieces, x_t = arrange((frames, slab_rows, cols), tp_count, shifts, *slabs)
    pieces, turned = lax.optimization_barrier((pieces, turned))
    full = lax.all_to_all(pieces, ("xh",) + TP, 0, 0, tiled=True)
    near0 = lax.all_gather(turned, "z8", axis=0, tiled=True)
    near0, theirs, full = lax.optimization_barrier((near0, theirs, full))
    pair1 = jnp.where(
        x_hi == 0,
        jnp.concatenate([mine, theirs], axis=0),
        jnp.concatenate([theirs, mine], axis=0),
    )
    gathered1 = lax.all_gather(pair1, ("z8", "z2", "c"), axis=0, tiled=False)
    z_count = sp_count // 2
    far0 = lax.ppermute(
        near0,
        ("z8", "z2", "c"),
        [(z * 2 + c, (z + 1 - 2 * c) % z_count * 2 + c) for z in range(z_count) for c in range(2)],
    )
    sums = run_block(
        First(frames, slab_rows, cols, total_rows), shifts,
        full.reshape(-1, shard_rows, half), qk_gain[0],
        [near0, far0, swap_cores(near0), swap_cores(far0)],
    )
    parts = lax.all_to_all(
        sums.reshape(2 * tp_count, local, half), ("xh",) + TP, 0, 0, tiled=True
    )
    x_t = add_up(x_t, parts)

    old_j = (pos_j - shifts[1, 1] + shifts[0, 1]) % cols
    x_t = exact(
        [(x_t, pick(pos_f, pos_r, pos_j, pos_f, pos_r, old_j))], (((1,), (0,)), ((), ()))
    )
    full = lax.all_to_all(
        spread([x_t[:, :half], x_t[:, half:]], tp_count // 2), TP, 0, 0, tiled=True
    )
    sums = run_block(
        Second(frames, slab_rows, cols, total_rows), shifts,
        full.reshape(-1, shard_rows, half), qk_gain[1],
        [gathered1.reshape(z_count, 2, 2 * shard_rows, 4 * head)],
    )
    parts = lax.all_to_all(sums.reshape(tp_count, local, half), TP, 0, 0, tiled=True)
    x_t = add_up(x_t, parts)

    new_j = (nat_w + shifts[1, 1]) % cols
    moved = nat_r + offset
    result = exact(
        [
            (pick(nat_f, moved - slab_rows * s, new_j, pos_f, pos_r, pos_j), slab)
            for s, slab in ((0, x_t), (1, neighbour(x_t, 1)), (-1, neighbour(x_t, -1)))
        ],
        NT,
    )
    return result.reshape(frames, slab_rows, cols, local)


def solution(mesh):
    shape = mesh.devices.shape
    fine = Mesh(mesh.devices.reshape(shape[0] // 4, 2, 2, 2, shape[1] // 4, 2), SP + TP)
    placed = (
        P(None, SP, None, TP),
        P(None, SP, None, TP),
        P(None, TP, SP),
        P(),
        P(),
        P(),
    )
    return jax.shard_map(
        on_device, mesh=fine, in_specs=placed, out_specs=P(None, SP, None, TP), check_vma=False
    )
```

```python
import functools
import math

import jax
import jax.numpy as jnp
from jax import lax
from jax.experimental import pallas as pl
from jax.experimental.pallas import tpu as pltpu
from jax.sharding import Mesh, PartitionSpec as P

WH = 4
WW = 8
UNITS = 4
CHUNKS = 4
TP = ("xl", "y", "c")
SP = ("z8", "z2", "xh")
NT = (((1,), (1,)), ((), ()))
TN = (((0,), (0,)), ((), ()))


def head_attention(projected, row_scale, qk_gain, same_window):
    width = projected.shape[1] // 3

    def normed(part, which):
        rows = projected[:, part * width : (part + 1) * width] * row_scale
        mean_square = jnp.mean(rows * rows, axis=-1, keepdims=True)
        return (rows * lax.rsqrt(mean_square + 1e-06) * qk_gain[which : which + 1, :]).astype(
            jnp.bfloat16
        )

    queries, key_rows = normed(0, 0), normed(1, 1)
    value_rows = (projected[:, 2 * width :] * row_scale).astype(jnp.bfloat16)
    scores = lax.dot_general(queries, key_rows, NT, preferred_element_type=jnp.float32)
    weights = jnp.where(same_window, jnp.exp(scores * (1.0 / math.sqrt(width))), 0.0)
    weights = (weights / jnp.sum(weights, axis=-1, keepdims=True)).astype(jnp.bfloat16)
    return jnp.dot(weights, value_rows, preferred_element_type=jnp.float32).astype(jnp.bfloat16)


def block_kernel(spec, weights_are_pairs, shifts, x_ref, qk_gain_ref, *refs):
    copies = []
    if weights_are_pairs:
        source, out_hbm, x_rows_ref, held_ref, x_held, out_ref, sems = refs
        weights = [held_ref]
        fetch = pltpu.make_async_copy(x_ref, x_held, sems.at[CHUNKS])
        fetch.start()
        x_ref = x_held
        size = source.shape[0] // CHUNKS
        for n in range(CHUNKS):
            there = slice(n * size, (n + 1) * size)
            copies.append(
                pltpu.make_async_copy(source.at[there], held_ref.at[there], sems.at[n])
            )
            copies[-1].start()
    else:
        weights, (out_ref, x_rows_ref) = refs[:-2], refs[-2:]
    slabs, units, rows, tokens = out_ref.shape
    heads = spec.heads
    windows = spec.windows
    head = qk_gain_ref.shape[1]
    step = UNITS * rows
    part = units // (CHUNKS if weights_are_pairs else len(weights))
    order = spec.order()
    shift_row, shift_col = shifts[spec.block, 0], shifts[spec.block, 1]
    first_rows = spec.first_rows(shifts)
    first_col = lax.axis_index("c") * spec.half_cols

    def weight(h, u, count, columns):
        if weights_are_pairs:
            per = weights[0].shape[2] // rows
            found = weights[0][u // per : (u + count) // per, h, :, columns]
            return found.reshape(count * rows, found.shape[-1])
        g, start = u // part, u % part * rows
        return weights[g][start : start + count * rows, columns]

    def window(first_row, axis):
        token = lax.broadcasted_iota(jnp.int32, (tokens, tokens), axis)
        col = first_col + lax.bitwise_and(token, spec.half_cols - 1)
        row = lax.bitwise_and(
            lax.shift_right_logical(token, spec.half_cols.bit_length() - 1), spec.slab_rows - 1
        )
        row = lax.bitwise_and(first_row + row, spec.total_rows - 1)
        col = jnp.where(col < shift_col, col + spec.total_cols, col)
        row_window = lax.shift_right_logical(row + shift_row, WH.bit_length() - 1)
        return row_window * 16 + lax.shift_right_logical(col, WW.bit_length() - 1)

    if copies:
        fetch.wait()
    sent = []
    scales = []
    for w in range(windows):
        squares = jnp.zeros((rows, tokens), jnp.float32)
        for k in range(units):
            block = x_ref[spec.unit(w, k)].astype(jnp.float32)
            squares = squares + block * block
        mean_square = jnp.sum(squares, axis=0, keepdims=True) * (1.0 / (units * rows))
        scales.append(jnp.broadcast_to(lax.rsqrt(mean_square + 1e-06), (8, tokens)).T[:, 0:1])
        for u in range(0, units, UNITS):
            block = jnp.concatenate(
                [x_ref[spec.unit(w, order[u + k])] for k in range(UNITS)], axis=0
            )
            x_rows_ref[w * tokens : (w + 1) * tokens, u * rows : u * rows + step] = block.T

    projected = [jnp.zeros((windows * tokens, 3 * head), jnp.float32)] * heads
    for u in range(0, units, part):
        if copies:
            copies[u // part].wait()
        for h in range(heads):
            projected[h] = projected[h] + jnp.dot(
                x_rows_ref[:, u * rows : (u + part) * rows],
                weight(h, u, part, slice(0, 3 * head)),
                preferred_element_type=jnp.float32,
            )
    attended = []
    for h in range(heads):
        of_window = []
        for w in range(windows):
            first_row = first_rows[w]
            of_window.append(
                head_attention(
                    projected[h][w * tokens : (w + 1) * tokens],
                    scales[w],
                    qk_gain_ref[...],
                    window(first_row, 0) == window(first_row, 1),
                )
            )
        if windows > slabs:
            frame = tokens // spec.frames
            of_window = [
                of_window[s + (q % 2)][
                    q // 2 * frame + (1 - q % 2) * frame // 2 :
                    q // 2 * frame + (2 - q % 2) * frame // 2
                ]
                for s in range(slabs)
                for q in range(2 * spec.frames)
            ]
        attended.append(jnp.concatenate(of_window, axis=0))
    for u in range(0, units, UNITS):
        total = jnp.zeros((step, slabs * tokens), jnp.float32)
        for h in range(heads):
            total = total + lax.dot_general(
                weight(h, u, UNITS, slice(3 * head, 4 * head)),
                attended[h],
                NT,
                preferred_element_type=jnp.float32,
            )
        total = total.astype(jnp.bfloat16)
        for slab in range(slabs):
            for k in range(UNITS):
                out_ref[slab, order[u + k]] = total[
                    k * rows : (k + 1) * rows, slab * tokens : (slab + 1) * tokens
                ]
        if copies:
            made = (slice(0, slabs), slice(u, u + UNITS))
            sent.append(
                pltpu.make_async_copy(
                    out_ref.at[made], out_hbm.at[made], sems.at[CHUNKS + 1 + u // UNITS]
                )
            )
            sent[-1].start()
    for copy in sent:
        copy.wait()


class Spec:
    def __init__(self, frames, slab_rows, cols, total_rows):
        self.frames, self.slab_rows, self.half_cols = frames, slab_rows, cols // 2
        self.total_rows, self.total_cols = total_rows, cols


def row_offset(shifts):
    return jnp.where(shifts[1, 0] > WH // 2, shifts[1, 0] - WH, shifts[1, 0])


class First(Spec):
    block, heads, windows, slabs = 0, 1, 3, 2

    def first_rows(self, shifts):
        z = lax.axis_index("z8") * 2 + lax.axis_index("z2")
        first = 2 * self.slab_rows * z - row_offset(shifts) - self.slab_rows // 2
        return [first + self.total_rows + w * self.slab_rows for w in range(self.windows)]

    def unit(self, w, k):
        owner, odd = k >> 1, k & 1
        if w == 1:
            return odd * 48 + owner * 3 + 2
        return (w // 2) * 48 + owner * 3 + odd

    def order(self):
        odd, core = lax.axis_index("z2"), lax.axis_index("c")
        return [
            (2 * m + z) * 2 + x for x in (core, 1 - core) for z in (odd, 1 - odd) for m in range(8)
        ]


class Second(Spec):
    block, heads, windows, slabs = 1, 2, 1, 1

    def first_rows(self, shifts):
        slab = (lax.axis_index("z8") * 2 + lax.axis_index("z2")) * 2 + lax.axis_index("xh")
        return [self.slab_rows * slab - row_offset(shifts) + self.total_rows]

    def unit(self, w, k):
        return k

    def order(self):
        return list(range(32))


def run_block(spec, shifts, x, qk_gain, weights):
    rows, tokens = x.shape[1:]
    units = sum(w.size for w in weights) // (spec.heads * rows * 4 * qk_gain.shape[1])
    scratch = [pltpu.VMEM((spec.windows * tokens, units * rows), jnp.bfloat16)]
    if len(weights) == 1:
        scratch += [
            pltpu.VMEM(weights[0].shape, jnp.bfloat16),
            pltpu.VMEM(x.shape, jnp.bfloat16),
            pltpu.VMEM((spec.slabs, units, rows, tokens), jnp.bfloat16),
            pltpu.SemaphoreType.DMA((CHUNKS + 1 + units // UNITS,)),
        ]
    vmem = pl.BlockSpec(memory_space=pltpu.VMEM)
    smem = pl.BlockSpec(memory_space=pltpu.SMEM)
    place = pl.BlockSpec(memory_space=pl.ANY) if len(weights) == 1 else vmem
    return pl.pallas_call(
        functools.partial(block_kernel, spec, len(weights) == 1),
        out_shape=jax.ShapeDtypeStruct((spec.slabs, units, rows, tokens), jnp.bfloat16),
        in_specs=[smem, place, vmem] + [place] * len(weights),
        out_specs=place,
        scratch_shapes=scratch,
        compiler_params=pltpu.CompilerParams(
            vmem_limit_bytes=(58 if len(weights) == 1 else 40) * 1024 * 1024
        ),
        cost_estimate=pl.CostEstimate(
            flops=2 * spec.windows * tokens * sum(w.size for w in weights),
            bytes_accessed=2 * sum(w.size for w in weights) + 4 * x.size,
            transcendentals=spec.heads * spec.windows * tokens * tokens,
        ),
        name="window_block",
    )(shifts, x, qk_gain, *weights)


def arrange_kernel(dims, copies, shifts, before_ref, own_ref, after_ref, pieces_ref, x_ref):
    frames, slab_rows, cols = dims
    count, local = own_ref.shape
    half, half_cols = count // 2, cols // 2
    x_hi = lax.axis_index("xh")
    tokens = jnp.concatenate([before_ref[...], own_ref[...], after_ref[...]], axis=0).T
    lane = lax.broadcasted_iota(jnp.int32, (1, count), 1)
    f = lax.bitwise_and(lax.div(lane, slab_rows * half_cols), frames - 1)
    r = lax.bitwise_and(lax.div(lane, half_cols), slab_rows - 1)
    j = lax.div(lane, half) * half_cols + lax.bitwise_and(lane, half_cols - 1)
    w = lax.bitwise_and(j - shifts[0, 1] + cols, cols - 1)

    def rows_from(start):
        row = start - row_offset(shifts) + r
        slab = lax.div(row, slab_rows)
        source = slab * count + f * (slab_rows * cols) + (row - slab * slab_rows) * cols + w
        hit = lax.broadcasted_iota(jnp.int32, (3 * count, count), 0) == source
        chosen = jnp.where(hit, 1.0, 0.0).astype(jnp.bfloat16)
        return jnp.dot(tokens, chosen, preferred_element_type=jnp.float32).astype(jnp.bfloat16)

    outer = rows_from(slab_rows // 2 + slab_rows * x_hi)
    middle = rows_from(slab_rows + slab_rows // 2 - slab_rows * x_hi)
    middle = jnp.where(x_hi == 0, middle[: local // 2], middle[local // 2 :])
    x_ref[...] = rows_from(slab_rows)
    for c in range(2):
        for i in range(copies):
            pieces_ref[2 * i + c, :local] = outer[:, c * half : (c + 1) * half]
            pieces_ref[2 * i + c, local:] = middle[:, c * half : (c + 1) * half]


def arrange(dims, copies, shifts, before, own, after):
    count, local = own.shape
    vmem = pl.BlockSpec(memory_space=pltpu.VMEM)
    return pl.pallas_call(
        functools.partial(arrange_kernel, dims, copies),
        out_shape=(
            jax.ShapeDtypeStruct((2 * copies, local + local // 2, count // 2), jnp.bfloat16),
            jax.ShapeDtypeStruct((local, count), jnp.bfloat16),
        ),
        in_specs=[pl.BlockSpec(memory_space=pltpu.SMEM)] + [vmem] * 3,
        out_specs=(vmem, vmem),
        compiler_params=pltpu.CompilerParams(vmem_limit_bytes=32 * 1024 * 1024),
        cost_estimate=pl.CostEstimate(
            flops=2 * local * 9 * count * count,
            bytes_accessed=2 * (copies + 4) * count * local,
            transcendentals=0,
        ),
        name="arrange_tokens",
    )(shifts, before, own, after)


def neighbour(x, distance):
    count = lax.axis_size(SP)
    return lax.ppermute(x, SP, [(i, (i - distance) % count) for i in range(count)])


def swap_cores(x):
    return lax.ppermute(x, "c", [(0, 1), (1, 0)])


def on_device(tokens, qkv_weight, out_weight, norm_gain, qk_gain, shifts):
    frames, slab_rows, cols, local = tokens.shape
    count = frames * slab_rows * cols
    half = count // 2
    half_cols = cols // 2
    tp_count = lax.axis_size(TP)
    head = qk_gain.shape[-1]
    shard_rows = out_weight.shape[-1]
    sp_count = lax.axis_size(SP)
    total_rows = slab_rows * sp_count
    sp_rank = lax.axis_index(SP)
    x_hi = lax.axis_index("xh")

    def shard(b):
        gain = lax.dynamic_slice_in_dim(norm_gain[b], sp_rank * shard_rows, shard_rows)
        scaled = qkv_weight[b].reshape(shard_rows, 3 * head).astype(jnp.float32) * gain[:, None]
        return jnp.concatenate([scaled.astype(jnp.bfloat16), out_weight[b].T], axis=1)

    turned = lax.ppermute(
        shard(0), ("xh", "c"), [(xh * 2 + c, c * 2 + xh) for xh in range(2) for c in range(2)]
    )
    mine = shard(1)
    theirs = lax.ppermute(mine, "xh", [(0, 1), (1, 0)])
    natural = tokens.reshape(count, local)
    slabs = [neighbour(natural, -1), natural, neighbour(natural, 1)]

    offset = row_offset(shifts)
    lane = jnp.arange(count, dtype=jnp.int32)
    nat_f, nat_r, nat_w = lane // (slab_rows * cols), lane // cols % slab_rows, lane % cols
    pos_f = lane // (slab_rows * half_cols) % frames
    pos_r = lane // half_cols % slab_rows
    pos_j = lane // half * half_cols + lane % half_cols

    def pick(rows_f, rows_r, rows_c, f, r, c):
        hit = (rows_f[:, None] == f[None]) & (rows_r[:, None] == r[None])
        return (hit & (rows_c[:, None] == c[None])).astype(jnp.bfloat16)

    def exact(terms, dims_):
        total = sum(
            lax.dot_general(a, b, dims_, preferred_element_type=jnp.float32) for a, b in terms
        )
        return total.astype(jnp.bfloat16)

    def spread(halves, copies):
        pieces = jnp.broadcast_to(jnp.stack(halves)[None], (copies, 2) + halves[0].shape)
        return pieces.reshape((copies * 2,) + halves[0].shape)

    def add_up(x_t, parts):
        parts = parts.reshape(-1, 2, local, half).astype(jnp.float32)
        total = jnp.sum(parts, axis=0)
        total = jnp.concatenate([total[0], total[1]], axis=1)
        return (x_t.astype(jnp.float32) + total).astype(jnp.bfloat16)

    pieces, x_t = arrange((frames, slab_rows, cols), tp_count, shifts, *slabs)
    pieces, turned = lax.optimization_barrier((pieces, turned))
    full = lax.all_to_all(pieces, ("xh",) + TP, 0, 0, tiled=True)
    near0 = lax.all_gather(turned, "z8", axis=0, tiled=True)
    near0, theirs, full = lax.optimization_barrier((near0, theirs, full))
    pair1 = jnp.where(
        x_hi == 0,
        jnp.concatenate([mine, theirs], axis=0),
        jnp.concatenate([theirs, mine], axis=0),
    )
    gathered1 = lax.all_gather(pair1, ("z8", "z2", "c"), axis=0, tiled=False)
    z_count = sp_count // 2
    far0 = lax.ppermute(
        near0,
        ("z8", "z2", "c"),
        [(z * 2 + c, (z + 1 - 2 * c) % z_count * 2 + c) for z in range(z_count) for c in range(2)],
    )
    sums = run_block(
        First(frames, slab_rows, cols, total_rows), shifts,
        full.reshape(-1, shard_rows, half), qk_gain[0],
        [near0, far0, swap_cores(near0), swap_cores(far0)],
    )
    parts = lax.all_to_all(
        sums.reshape(2 * tp_count, local, half), ("xh",) + TP, 0, 0, tiled=True
    )
    x_t = add_up(x_t, parts)

    old_j = (pos_j - shifts[1, 1] + shifts[0, 1]) % cols
    x_t = exact(
        [(x_t, pick(pos_f, pos_r, pos_j, pos_f, pos_r, old_j))], (((1,), (0,)), ((), ()))
    )
    full = lax.all_to_all(
        spread([x_t[:, :half], x_t[:, half:]], tp_count // 2), TP, 0, 0, tiled=True
    )
    sums = run_block(
        Second(frames, slab_rows, cols, total_rows), shifts,
        full.reshape(-1, shard_rows, half), qk_gain[1],
        [gathered1.reshape(z_count, 2, 2 * shard_rows, 4 * head)],
    )
    parts = lax.all_to_all(sums.reshape(tp_count, local, half), TP, 0, 0, tiled=True)
    x_t = add_up(x_t, parts)

    side = jnp.where(offset > 0, 2, jnp.where(offset < 0, 0, 1))
    beside = lax.switch(
        side, [lambda x: neighbour(x, -1), lambda x: x, lambda x: neighbour(x, 1)], x_t
    )
    new_j = (nat_w + shifts[1, 1]) % cols
    moved = nat_r + offset
    in_beside = jnp.where(offset < 0, moved + slab_rows, moved - slab_rows)
    result = exact(
        [
            (pick(nat_f, moved, new_j, pos_f, pos_r, pos_j), x_t),
            (pick(nat_f, in_beside, new_j, pos_f, pos_r, pos_j), beside),
        ],
        NT,
    )
    return result.reshape(frames, slab_rows, cols, local)


def solution(mesh):
    shape = mesh.devices.shape
    fine = Mesh(mesh.devices.reshape(shape[0] // 4, 2, 2, 2, shape[1] // 4, 2), SP + TP)
    placed = (
        P(None, SP, None, TP),
        P(None, SP, None, TP),
        P(None, TP, SP),
        P(),
        P(),
        P(),
    )
    return jax.shard_map(
        on_device, mesh=fine, in_specs=placed, out_specs=P(None, SP, None, TP), check_vma=False
    )
```

```python
import functools
import math

import jax
import jax.numpy as jnp
from jax import lax
from jax.experimental import pallas as pl
from jax.experimental.pallas import tpu as pltpu
from jax.sharding import Mesh, PartitionSpec as P

WH = 4
WW = 8
UNITS = 4
CHUNKS = 2
TP = ("xl", "y", "c")
SP = ("z8", "z2", "xh")
NT = (((1,), (1,)), ((), ()))
TN = (((0,), (0,)), ((), ()))


def head_attention(projected, row_scale, qk_gain, same_window):
    width = projected.shape[1] // 3

    def normed(part, which):
        rows = projected[:, part * width : (part + 1) * width] * row_scale
        mean_square = jnp.mean(rows * rows, axis=-1, keepdims=True)
        return (rows * lax.rsqrt(mean_square + 1e-06) * qk_gain[which : which + 1, :]).astype(
            jnp.bfloat16
        )

    queries, key_rows = normed(0, 0), normed(1, 1)
    value_rows = (projected[:, 2 * width :] * row_scale).astype(jnp.bfloat16)
    scores = lax.dot_general(queries, key_rows, NT, preferred_element_type=jnp.float32)
    weights = jnp.where(same_window, jnp.exp(scores * (1.0 / math.sqrt(width))), 0.0)
    weights = (weights / jnp.sum(weights, axis=-1, keepdims=True)).astype(jnp.bfloat16)
    return jnp.dot(weights, value_rows, preferred_element_type=jnp.float32).astype(jnp.bfloat16)


def block_kernel(spec, weights_are_pairs, shifts, x_ref, qk_gain_ref, *refs):
    copies = []
    if weights_are_pairs:
        source, out_hbm, x_rows_ref, held_ref, x_held, out_ref, sems = refs
        weights = [held_ref]
        fetch = pltpu.make_async_copy(x_ref, x_held, sems.at[CHUNKS])
        fetch.start()
        x_ref = x_held
        size = source.shape[0] // CHUNKS
        for n in range(CHUNKS):
            there = slice(n * size, (n + 1) * size)
            copies.append(
                pltpu.make_async_copy(source.at[there], held_ref.at[there], sems.at[n])
            )
            copies[-1].start()
    else:
        weights, (out_ref, x_rows_ref) = refs[:-2], refs[-2:]
    slabs, units, rows, tokens = out_ref.shape
    heads = spec.heads
    windows = spec.windows
    head = qk_gain_ref.shape[1]
    step = UNITS * rows
    part = units // (CHUNKS if weights_are_pairs else len(weights))
    order = spec.order()
    shift_row, shift_col = shifts[spec.block, 0], shifts[spec.block, 1]
    first_rows = spec.first_rows(shifts)
    first_col = lax.axis_index("c") * spec.half_cols

    def weight(h, u, count, columns):
        if weights_are_pairs:
            per = weights[0].shape[2] // rows
            found = weights[0][u // per : (u + count) // per, h, :, columns]
            return found.reshape(count * rows, found.shape[-1])
        g, start = u // part, u % part * rows
        return weights[g][start : start + count * rows, columns]

    def window(first_row, axis):
        token = lax.broadcasted_iota(jnp.int32, (tokens, tokens), axis)
        col = first_col + lax.bitwise_and(token, spec.half_cols - 1)
        row = lax.bitwise_and(
            lax.shift_right_logical(token, spec.half_cols.bit_length() - 1), spec.slab_rows - 1
        )
        row = lax.bitwise_and(first_row + row, spec.total_rows - 1)
        col = jnp.where(col < shift_col, col + spec.total_cols, col)
        row_window = lax.shift_right_logical(row + shift_row, WH.bit_length() - 1)
        return row_window * 16 + lax.shift_right_logical(col, WW.bit_length() - 1)

    if copies:
        fetch.wait()
    sent = []
    scales = []
    for w in range(windows):
        squares = jnp.zeros((rows, tokens), jnp.float32)
        for k in range(units):
            block = x_ref[spec.unit(w, k)].astype(jnp.float32)
            squares = squares + block * block
        mean_square = jnp.sum(squares, axis=0, keepdims=True) * (1.0 / (units * rows))
        scales.append(jnp.broadcast_to(lax.rsqrt(mean_square + 1e-06), (8, tokens)).T[:, 0:1])
        for u in range(0, units, UNITS):
            block = jnp.concatenate(
                [x_ref[spec.unit(w, order[u + k])] for k in range(UNITS)], axis=0
            )
            x_rows_ref[w * tokens : (w + 1) * tokens, u * rows : u * rows + step] = block.T

    projected = [jnp.zeros((windows * tokens, 3 * head), jnp.float32)] * heads
    for u in range(0, units, part):
        if copies:
            copies[u // part].wait()
        for h in range(heads):
            projected[h] = projected[h] + jnp.dot(
                x_rows_ref[:, u * rows : (u + part) * rows],
                weight(h, u, part, slice(0, 3 * head)),
                preferred_element_type=jnp.float32,
            )
    attended = []
    for h in range(heads):
        of_window = []
        for w in range(windows):
            first_row = first_rows[w]
            of_window.append(
                head_attention(
                    projected[h][w * tokens : (w + 1) * tokens],
                    scales[w],
                    qk_gain_ref[...],
                    window(first_row, 0) == window(first_row, 1),
                )
            )
        if windows > slabs:
            frame = tokens // spec.frames
            of_window = [
                of_window[s + (q % 2)][
                    q // 2 * frame + (1 - q % 2) * frame // 2 :
                    q // 2 * frame + (2 - q % 2) * frame // 2
                ]
                for s in range(slabs)
                for q in range(2 * spec.frames)
            ]
        attended.append(jnp.concatenate(of_window, axis=0))
    for u in range(0, units, UNITS):
        total = jnp.zeros((step, slabs * tokens), jnp.float32)
        for h in range(heads):
            total = total + lax.dot_general(
                weight(h, u, UNITS, slice(3 * head, 4 * head)),
                attended[h],
                NT,
                preferred_element_type=jnp.float32,
            )
        total = total.astype(jnp.bfloat16)
        for slab in range(slabs):
            for k in range(UNITS):
                out_ref[slab, order[u + k]] = total[
                    k * rows : (k + 1) * rows, slab * tokens : (slab + 1) * tokens
                ]
        if copies:
            made = (slice(0, slabs), slice(u, u + UNITS))
            sent.append(
                pltpu.make_async_copy(
                    out_ref.at[made], out_hbm.at[made], sems.at[CHUNKS + 1 + u // UNITS]
                )
            )
            sent[-1].start()
    for copy in sent:
        copy.wait()


class Spec:
    def __init__(self, frames, slab_rows, cols, total_rows):
        self.frames, self.slab_rows, self.half_cols = frames, slab_rows, cols // 2
        self.total_rows, self.total_cols = total_rows, cols


def row_offset(shifts):
    return jnp.where(shifts[1, 0] > WH // 2, shifts[1, 0] - WH, shifts[1, 0])


class First(Spec):
    block, heads, windows, slabs = 0, 1, 3, 2

    def first_rows(self, shifts):
        z = lax.axis_index("z8") * 2 + lax.axis_index("z2")
        first = 2 * self.slab_rows * z - row_offset(shifts) - self.slab_rows // 2
        return [first + self.total_rows + w * self.slab_rows for w in range(self.windows)]

    def unit(self, w, k):
        owner, odd = k >> 1, k & 1
        if w == 1:
            return odd * 48 + owner * 3 + 2
        return (w // 2) * 48 + owner * 3 + odd

    def order(self):
        odd, core = lax.axis_index("z2"), lax.axis_index("c")
        return [
            (2 * m + z) * 2 + x for x in (core, 1 - core) for z in (odd, 1 - odd) for m in range(8)
        ]


class Second(Spec):
    block, heads, windows, slabs = 1, 2, 1, 1

    def first_rows(self, shifts):
        slab = (lax.axis_index("z8") * 2 + lax.axis_index("z2")) * 2 + lax.axis_index("xh")
        return [self.slab_rows * slab - row_offset(shifts) + self.total_rows]

    def unit(self, w, k):
        return k

    def order(self):
        return list(range(32))


def run_block(spec, shifts, x, qk_gain, weights):
    rows, tokens = x.shape[1:]
    units = sum(w.size for w in weights) // (spec.heads * rows * 4 * qk_gain.shape[1])
    scratch = [pltpu.VMEM((spec.windows * tokens, units * rows), jnp.bfloat16)]
    if len(weights) == 1:
        scratch += [
            pltpu.VMEM(weights[0].shape, jnp.bfloat16),
            pltpu.VMEM(x.shape, jnp.bfloat16),
            pltpu.VMEM((spec.slabs, units, rows, tokens), jnp.bfloat16),
            pltpu.SemaphoreType.DMA((CHUNKS + 1 + units // UNITS,)),
        ]
    vmem = pl.BlockSpec(memory_space=pltpu.VMEM)
    smem = pl.BlockSpec(memory_space=pltpu.SMEM)
    place = pl.BlockSpec(memory_space=pl.ANY) if len(weights) == 1 else vmem
    return pl.pallas_call(
        functools.partial(block_kernel, spec, len(weights) == 1),
        out_shape=jax.ShapeDtypeStruct((spec.slabs, units, rows, tokens), jnp.bfloat16),
        in_specs=[smem, place, vmem] + [place] * len(weights),
        out_specs=place,
        scratch_shapes=scratch,
        compiler_params=pltpu.CompilerParams(
            vmem_limit_bytes=(58 if len(weights) == 1 else 40) * 1024 * 1024
        ),
        cost_estimate=pl.CostEstimate(
            flops=2 * spec.windows * tokens * sum(w.size for w in weights),
            bytes_accessed=2 * sum(w.size for w in weights) + 4 * x.size,
            transcendentals=spec.heads * spec.windows * tokens * tokens,
        ),
        name="window_block",
    )(shifts, x, qk_gain, *weights)


def arrange_kernel(dims, copies, shifts, before_ref, own_ref, after_ref, pieces_ref, x_ref):
    frames, slab_rows, cols = dims
    count, local = own_ref.shape
    half, half_cols = count // 2, cols // 2
    x_hi = lax.axis_index("xh")
    tokens = jnp.concatenate([before_ref[...], own_ref[...], after_ref[...]], axis=0).T
    lane = lax.broadcasted_iota(jnp.int32, (1, count), 1)
    f = lax.bitwise_and(lax.div(lane, slab_rows * half_cols), frames - 1)
    r = lax.bitwise_and(lax.div(lane, half_cols), slab_rows - 1)
    j = lax.div(lane, half) * half_cols + lax.bitwise_and(lane, half_cols - 1)
    w = lax.bitwise_and(j - shifts[0, 1] + cols, cols - 1)

    def rows_from(start):
        row = start - row_offset(shifts) + r
        slab = lax.div(row, slab_rows)
        source = slab * count + f * (slab_rows * cols) + (row - slab * slab_rows) * cols + w
        hit = lax.broadcasted_iota(jnp.int32, (3 * count, count), 0) == source
        chosen = jnp.where(hit, 1.0, 0.0).astype(jnp.bfloat16)
        return jnp.dot(tokens, chosen, preferred_element_type=jnp.float32).astype(jnp.bfloat16)

    outer = rows_from(slab_rows // 2 + slab_rows * x_hi)
    middle = rows_from(slab_rows + slab_rows // 2 - slab_rows * x_hi)
    middle = jnp.where(x_hi == 0, middle[: local // 2], middle[local // 2 :])
    x_ref[...] = rows_from(slab_rows)
    for c in range(2):
        for i in range(copies):
            pieces_ref[2 * i + c, :local] = outer[:, c * half : (c + 1) * half]
            pieces_ref[2 * i + c, local:] = middle[:, c * half : (c + 1) * half]


def arrange(dims, copies, shifts, before, own, after):
    count, local = own.shape
    vmem = pl.BlockSpec(memory_space=pltpu.VMEM)
    return pl.pallas_call(
        functools.partial(arrange_kernel, dims, copies),
        out_shape=(
            jax.ShapeDtypeStruct((2 * copies, local + local // 2, count // 2), jnp.bfloat16),
            jax.ShapeDtypeStruct((local, count), jnp.bfloat16),
        ),
        in_specs=[pl.BlockSpec(memory_space=pltpu.SMEM)] + [vmem] * 3,
        out_specs=(vmem, vmem),
        compiler_params=pltpu.CompilerParams(vmem_limit_bytes=32 * 1024 * 1024),
        cost_estimate=pl.CostEstimate(
            flops=2 * local * 9 * count * count,
            bytes_accessed=2 * (copies + 4) * count * local,
            transcendentals=0,
        ),
        name="arrange_tokens",
    )(shifts, before, own, after)


def neighbour(x, distance):
    count = lax.axis_size(SP)
    return lax.ppermute(x, SP, [(i, (i - distance) % count) for i in range(count)])


def swap_cores(x):
    return lax.ppermute(x, "c", [(0, 1), (1, 0)])


def on_device(tokens, qkv_weight, out_weight, norm_gain, qk_gain, shifts):
    frames, slab_rows, cols, local = tokens.shape
    count = frames * slab_rows * cols
    half = count // 2
    half_cols = cols // 2
    tp_count = lax.axis_size(TP)
    head = qk_gain.shape[-1]
    shard_rows = out_weight.shape[-1]
    sp_count = lax.axis_size(SP)
    total_rows = slab_rows * sp_count
    sp_rank = lax.axis_index(SP)
    x_hi = lax.axis_index("xh")

    def shard(b):
        gain = lax.dynamic_slice_in_dim(norm_gain[b], sp_rank * shard_rows, shard_rows)
        scaled = qkv_weight[b].reshape(shard_rows, 3 * head).astype(jnp.float32) * gain[:, None]
        return jnp.concatenate([scaled.astype(jnp.bfloat16), out_weight[b].T], axis=1)

    turned = lax.ppermute(
        shard(0), ("xh", "c"), [(xh * 2 + c, c * 2 + xh) for xh in range(2) for c in range(2)]
    )
    mine = shard(1)
    theirs = lax.ppermute(mine, "xh", [(0, 1), (1, 0)])
    natural = tokens.reshape(count, local)
    slabs = [neighbour(natural, -1), natural, neighbour(natural, 1)]

    offset = row_offset(shifts)
    lane = jnp.arange(count, dtype=jnp.int32)
    nat_f, nat_r, nat_w = lane // (slab_rows * cols), lane // cols % slab_rows, lane % cols
    pos_f = lane // (slab_rows * half_cols) % frames
    pos_r = lane // half_cols % slab_rows
    pos_j = lane // half * half_cols + lane % half_cols

    def pick(rows_f, rows_r, rows_c, f, r, c):
        hit = (rows_f[:, None] == f[None]) & (rows_r[:, None] == r[None])
        return (hit & (rows_c[:, None] == c[None])).astype(jnp.bfloat16)

    def exact(terms, dims_):
        total = sum(
            lax.dot_general(a, b, dims_, preferred_element_type=jnp.float32) for a, b in terms
        )
        return total.astype(jnp.bfloat16)

    def spread(halves, copies):
        pieces = jnp.broadcast_to(jnp.stack(halves)[None], (copies, 2) + halves[0].shape)
        return pieces.reshape((copies * 2,) + halves[0].shape)

    def add_up(x_t, parts):
        parts = parts.reshape(-1, 2, local, half).astype(jnp.float32)
        total = jnp.sum(parts, axis=0)
        total = jnp.concatenate([total[0], total[1]], axis=1)
        return (x_t.astype(jnp.float32) + total).astype(jnp.bfloat16)

    pieces, x_t = arrange((frames, slab_rows, cols), tp_count, shifts, *slabs)
    pieces, turned = lax.optimization_barrier((pieces, turned))
    full = lax.all_to_all(pieces, ("xh",) + TP, 0, 0, tiled=True)
    near0 = lax.all_gather(turned, "z8", axis=0, tiled=True)
    near0, theirs, full = lax.optimization_barrier((near0, theirs, full))
    pair1 = jnp.where(
        x_hi == 0,
        jnp.concatenate([mine, theirs], axis=0),
        jnp.concatenate([theirs, mine], axis=0),
    )
    gathered1 = lax.all_gather(pair1, ("z8", "z2", "c"), axis=0, tiled=False)
    z_count = sp_count // 2
    far0 = lax.ppermute(
        near0,
        ("z8", "z2", "c"),
        [(z * 2 + c, (z + 1 - 2 * c) % z_count * 2 + c) for z in range(z_count) for c in range(2)],
    )
    sums = run_block(
        First(frames, slab_rows, cols, total_rows), shifts,
        full.reshape(-1, shard_rows, half), qk_gain[0],
        [near0, far0, swap_cores(near0), swap_cores(far0)],
    )
    parts = lax.all_to_all(
        sums.reshape(2 * tp_count, local, half), ("xh",) + TP, 0, 0, tiled=True
    )
    x_t = add_up(x_t, parts)

    old_j = (pos_j - shifts[1, 1] + shifts[0, 1]) % cols
    x_t = exact(
        [(x_t, pick(pos_f, pos_r, pos_j, pos_f, pos_r, old_j))], (((1,), (0,)), ((), ()))
    )
    full = lax.all_to_all(
        spread([x_t[:, :half], x_t[:, half:]], tp_count // 2), TP, 0, 0, tiled=True
    )
    sums = run_block(
        Second(frames, slab_rows, cols, total_rows), shifts,
        full.reshape(-1, shard_rows, half), qk_gain[1],
        [gathered1.reshape(z_count, 2, 2 * shard_rows, 4 * head)],
    )
    parts = lax.all_to_all(sums.reshape(tp_count, local, half), TP, 0, 0, tiled=True)
    x_t = add_up(x_t, parts)

    side = jnp.where(offset > 0, 2, jnp.where(offset < 0, 0, 1))
    beside = lax.switch(
        side, [lambda x: neighbour(x, -1), lambda x: x, lambda x: neighbour(x, 1)], x_t
    )
    new_j = (nat_w + shifts[1, 1]) % cols
    moved = nat_r + offset
    in_beside = jnp.where(offset < 0, moved + slab_rows, moved - slab_rows)
    result = exact(
        [
            (pick(nat_f, moved, new_j, pos_f, pos_r, pos_j), x_t),
            (pick(nat_f, in_beside, new_j, pos_f, pos_r, pos_j), beside),
        ],
        NT,
    )
    return result.reshape(frames, slab_rows, cols, local)


def solution(mesh):
    shape = mesh.devices.shape
    fine = Mesh(mesh.devices.reshape(shape[0] // 4, 2, 2, 2, shape[1] // 4, 2), SP + TP)
    placed = (
        P(None, SP, None, TP),
        P(None, SP, None, TP),
        P(None, TP, SP),
        P(),
        P(),
        P(),
    )
    return jax.shard_map(
        on_device, mesh=fine, in_specs=placed, out_specs=P(None, SP, None, TP), check_vma=False
    )
```
